32 devices in a mesh: kv: 8 (over y, x, core), dp: 4 (over z).
Axes of the slice: x: 2, y: 2, z: 4, core: 2. Of those that a mesh axis runs over, the one named last changes fastest.
Arguments:
- queries: bfloat16 [32, 128, 576], P('dp'), may hold values from -48 to 48
- drafts: bfloat16 [32, 576], P('dp'), may hold values from -18 to 18
- cache: bfloat16 [8, 32768, 576], P('dp', 'kv'), may hold values from -4 to 4
- lengths: int32 [8], P('dp'), may hold values from 16384 to 32768, as said below
- row_seq: int32 [32], P('dp'), may hold values from 0 to 1, as said below
- row_pos: int32 [32], P('dp'), may hold values from 16384 to 32771, as said below
- w_uv: bfloat16 [128, 512, 128], P('kv'), may hold values from -0.25 to 0.25
- w_out: bfloat16 [16384, 7168], P('kv', 'dp'), may hold values from -0.046875 to 0.046875
- hidden: bfloat16 [32, 7168], P(None, 'dp'), may hold values from -0.59765625 to 0.59765625
- gain: float32 [7168], P('dp'), may hold values from 0.1 to 1.9
- w_gate: bfloat16 [7168, 18432], P('dp', 'kv'), may hold values from -0.0625 to 0.0625
- w_up: bfloat16 [7168, 18432], P('dp', 'kv'), may hold values from -0.0625 to 0.0625
- w_down: bfloat16 [18432, 7168], P('kv', 'dp'), may hold values from -0.01171875 to 0.01171875
Outputs:
- mixed: bfloat16 [32, 7168], P(None, 'dp')
The draws below stay inside these ranges and needn't reach their ends.
Inputs may be any that keep to these rules, and one draw needn't show every extreme that they name: `lengths`: sequence 0 has exactly 32768 live positions. `row_seq`: each of a group's 2 sequences owns exactly 4 rows of the group, in any order. `row_pos`: A row's position is its sequence's length plus a step number; the 4 rows of one sequence take the step numbers 0 to 3 once each.
All inputs are finite; a program needn't handle non-finite values.
Results may differ from the reference program's by a relative error of at most 0.009.
Values may be sent and summed in bfloat16 or wider, within the bound.
No kernel may reach another device: no remote copies, remote signals or barrier semaphores. Data moves between devices by JAX's collectives and lax.ppermute only.
A program may use at most 128 MiB of HBM per device.

```python
import jax
import jax.numpy as jnp
from jax import lax

D = 7168
H = 128
LAT = 512
ROPE = 64
HD = 128
FF = 18432
SEQ_DP = 2
STEPS = 4
CTX = 32768
TOKENS = 32
N_DP = 4


def layout(key):
    keys_all = jax.random.split(key, 5)
    seq_total = SEQ_DP * N_DP
    tok_group = SEQ_DP * STEPS
    lengths = jax.random.randint(keys_all[0], (seq_total,), CTX // 2, CTX + 1).at[0].set(CTX)
    orders = jax.vmap(lambda sub: jax.random.permutation(sub, tok_group))(jax.random.split(keys_all[1], N_DP))
    seq_local = orders // STEPS
    step_num = orders % STEPS
    seq_global = jnp.arange(N_DP)[:, None] * SEQ_DP + seq_local
    positions = lengths[seq_global] + step_num
    offsets = jax.random.randint(keys_all[2], (seq_total,), 0, CTX // (4 * STEPS))
    spots = 2 * step_num + 2 * STEPS * offsets[seq_global]
    aligned = jnp.clip(jax.random.normal(keys_all[3], (tok_group * N_DP, LAT + ROPE)), -4.0, 4.0)
    aligned = aligned.astype(jnp.bfloat16).astype(jnp.float32)
    return (lengths, seq_local.reshape(-1), positions.reshape(-1), seq_global.reshape(-1), spots.reshape(-1), aligned, keys_all[4])


def draw_lengths(key, part):
    shared = layout(key)
    return shared[0].astype(jnp.int32)


def draw_row_seq(key, part):
    shared = layout(key)
    return shared[1].astype(jnp.int32)


def draw_row_pos(key, part):
    shared = layout(key)
    return shared[2].astype(jnp.int32)


def draw_cache(key, part):
    key = jax.random.fold_in(key, 11)
    base = jnp.clip(jax.random.normal(key, (SEQ_DP * N_DP, CTX, LAT + ROPE)), -4.0, 4.0)
    return base.astype(jnp.bfloat16)


def draw_queries(key, part):
    key = jax.random.fold_in(key, 13)
    row_total = SEQ_DP * STEPS * N_DP
    base = jnp.clip(1.5 * jax.random.normal(key, (row_total, H, LAT + ROPE)), -9.0, 9.0)
    return base.astype(jnp.bfloat16)


def shard_levels(stream_key, shape, cuts, low, top_value):
    level = 1.0
    for axis_at, shards_of in cuts:
        heights = jax.random.uniform(jax.random.fold_in(jax.random.fold_in(stream_key, 6), axis_at), (shards_of,), jnp.float32, low / len(cuts), top_value / len(cuts))
        level = level * jnp.repeat(jnp.exp(heights), shape[axis_at] // shards_of).reshape((-1,) + (1,) * (len(shape) - 1 - axis_at))
    return level


def gaussian(rng, extent, width, most, cuts=(), kind=jnp.bfloat16):
    entries = jax.random.normal(rng, extent, jnp.float32) * width
    if len(cuts) > 0:
        entries = shard_levels(rng, extent, cuts, -0.22, 0.18) * entries
    return jnp.clip(entries, min=-most, max=most).astype(kind)


def setup_inputs(seed: int = 0) -> dict:
    arg_keys = jax.random.split(jax.random.key(seed), 14)
    return {
        "queries": draw_queries(jax.random.fold_in(arg_keys[13], 71), 0),
        "drafts": gaussian(arg_keys[1], (TOKENS, LAT + ROPE), 3.0, 18.0, ((0, 4),)),
        "cache": draw_cache(jax.random.fold_in(arg_keys[13], 71), 0),
        "lengths": draw_lengths(jax.random.fold_in(arg_keys[13], 71), 0),
        "row_seq": draw_row_seq(jax.random.fold_in(arg_keys[13], 71), 0),
        "row_pos": draw_row_pos(jax.random.fold_in(arg_keys[13], 71), 0),
        "w_uv": gaussian(arg_keys[6], (H, LAT, HD), LAT ** -0.5, 0.25, ((0, 8),)),
        "w_out": gaussian(arg_keys[7], (H * HD, D), (H * HD) ** -0.5, 0.046875, ((0, 8), (1, 4))),
        "hidden": gaussian(arg_keys[8], (TOKENS, D), 0.1, 0.59765625, ((1, 4),)),
        "gain": jnp.clip(1.0 + 0.18 * jax.random.normal(arg_keys[9], (D,), jnp.float32), 0.1, 1.9),
        "w_gate": gaussian(arg_keys[10], (D, FF), D ** -0.5, 0.0625, ((0, 4), (1, 8))),
        "w_up": gaussian(arg_keys[11], (D, FF), D ** -0.5, 0.0625, ((0, 4), (1, 8))),
        "w_down": gaussian(arg_keys[12], (FF, D), (16 * FF) ** -0.5, 0.01171875, ((0, 8), (1, 4))),
    }


def attend_row(token, queries, drafts, cache, lengths, row_seq, row_pos):
    tok_group = SEQ_DP * STEPS
    group = token // tok_group
    seq_local = row_seq[token]
    seq_global = (group * SEQ_DP + seq_local).astype(jnp.int32)
    key_rows = lax.dynamic_index_in_dim(cache, seq_global, 0, keepdims=False)
    query = queries[token]
    qk_scale = (HD + ROPE) ** (-0.5)
    cache_scores = jnp.dot(query, key_rows.T, preferred_element_type=jnp.float32) * qk_scale
    cache_valid = jnp.arange(CTX, dtype=jnp.int32) < lengths[seq_global]
    group_start = (group * tok_group).astype(jnp.int32)
    draft_rows = lax.dynamic_slice_in_dim(drafts, group_start, tok_group, 0)
    draft_seq = lax.dynamic_slice_in_dim(row_seq, group_start, tok_group, 0)
    draft_pos = lax.dynamic_slice_in_dim(row_pos, group_start, tok_group, 0)
    draft_valid = (draft_seq == seq_local) & (draft_pos <= row_pos[token])
    draft_scores = jnp.dot(query, draft_rows.T, preferred_element_type=jnp.float32) * qk_scale
    lowest = -jnp.inf
    peak = jnp.maximum(lax.optimization_barrier(jnp.max(jnp.where(cache_valid[None, :], cache_scores, lowest), axis=1)), lax.optimization_barrier(jnp.max(jnp.where(draft_valid[None, :], draft_scores, lowest), axis=1)))
    cache_weight = jnp.where(cache_valid[None, :], jnp.exp(cache_scores - peak[:, None]), 0.0)
    draft_weight = jnp.where(draft_valid[None, :], jnp.exp(draft_scores - peak[:, None]), 0.0)
    denom = lax.optimization_barrier(jnp.sum(cache_weight, axis=1)) + lax.optimization_barrier(jnp.sum(draft_weight, axis=1))
    numer = jnp.dot(cache_weight.astype(jnp.bfloat16), key_rows[:, :LAT], preferred_element_type=jnp.float32)
    numer = numer + jnp.dot(draft_weight.astype(jnp.bfloat16), draft_rows[:, :LAT], preferred_element_type=jnp.float32)
    return (numer / denom[:, None]).astype(jnp.bfloat16)

def reference(queries, drafts, cache, lengths, row_seq, row_pos, w_uv, w_out, hidden, gain, w_gate, w_up, w_down):
    latent_out = lax.map(lambda token: attend_row(token, queries, drafts, cache, lengths, row_seq, row_pos), jnp.arange(TOKENS, dtype=jnp.int32))
    values = jnp.einsum('thl,hlv->thv', latent_out.astype(jnp.float32), w_uv.astype(jnp.float32)).astype(jnp.bfloat16)
    attended = jnp.dot(values.reshape(TOKENS, H * HD), w_out, preferred_element_type=jnp.float32)
    resid = (hidden.astype(jnp.float32) + attended).astype(jnp.bfloat16)
    resid_f = resid.astype(jnp.float32)
    inv_rms = lax.rsqrt(lax.optimization_barrier(jnp.mean(resid_f * resid_f, axis=1, keepdims=True)) + 1e-06)
    scaled = (resid_f * gain[None, :]).astype(jnp.bfloat16)
    gate = jnp.dot(scaled, w_gate, preferred_element_type=jnp.float32) * inv_rms
    up_val = jnp.dot(scaled, w_up, preferred_element_type=jnp.float32) * inv_rms
    act = (jax.nn.silu(gate) * up_val).astype(jnp.bfloat16)
    mixed = resid_f + jnp.dot(act, w_down, preferred_element_type=jnp.float32)
    return mixed.astype(jnp.bfloat16)
```

```python
import functools

import jax
import jax.numpy as jnp
from jax import lax
from jax.experimental import pallas as pl
from jax.experimental.pallas import tpu as pltpu
from jax.sharding import PartitionSpec as P

D = 7168
LAT = 512
ROPE = 64
HD = 128
SEQ_DP = 2
STEPS = 4


def scan_cache(query_rows, key_rows, live_len, block_len, block_count):
    qk_scale = (HD + ROPE) ** (-0.5)
    row_count = query_rows.shape[0]

    def visit(block_idx, carry):
        run_max, run_sum, weighted = carry
        key_block = lax.dynamic_slice_in_dim(key_rows, block_idx * block_len, block_len, 0)
        scores = (
            jnp.einsum("rc,kc->rk", query_rows, key_block, preferred_element_type=jnp.float32)
            * qk_scale
        )
        valid = block_idx * block_len + jnp.arange(block_len) < live_len
        scores = jnp.where(valid[None, :], scores, -1e30)
        new_max = jnp.maximum(run_max, jnp.max(scores, axis=1))
        weights = jnp.where(valid[None, :], jnp.exp(scores - new_max[:, None]), 0.0)
        factor = jnp.exp(run_max - new_max)
        run_sum = run_sum * factor + jnp.sum(weights, axis=1)
        weighted = weighted * factor[:, None] + jnp.dot(
            weights.astype(jnp.bfloat16), key_block[:, :LAT], preferred_element_type=jnp.float32
        )
        return (new_max, run_sum, weighted)

    start_carry = (
        jnp.full((row_count,), -1e30, jnp.float32),
        jnp.zeros((row_count,), jnp.float32),
        jnp.zeros((row_count, LAT), jnp.float32),
    )
    return lax.fori_loop(0, block_count, visit, start_carry)


def on_device(
    queries,
    drafts,
    cache,
    lengths,
    row_seq,
    row_pos,
    w_uv,
    w_out,
    hidden,
    gain,
    w_gate,
    w_up,
    w_down,
):
    kv_count = lax.axis_size("kv")
    kv_index = lax.axis_index("kv")
    tok_group, head_count = (queries.shape[0], queries.shape[1])
    head_local = head_count // kv_count
    ctx_dev = cache.shape[1]
    shard_start = kv_index * ctx_dev
    block_len = min(512, ctx_dev)
    block_total = ctx_dev // block_len
    qk_scale = (HD + ROPE) ** (-0.5)
    order_idx = jnp.arange(tok_group)
    same_seq = row_seq[:, None] == row_seq[None, :]
    rank_in_seq = jnp.sum(same_seq & (order_idx[:, None] > order_idx[None, :]), axis=1)
    picker = (row_seq[None, None, :] == jnp.arange(SEQ_DP)[:, None, None]) & (
        rank_in_seq[None, None, :] == jnp.arange(STEPS)[None, :, None]
    )
    picker_b = picker.astype(jnp.bfloat16)
    sorted_q = jnp.einsum(
        "sri,ihc->srhc", picker_b, queries, preferred_element_type=jnp.float32
    ).astype(jnp.bfloat16)
    sorted_drafts = (
        jnp.einsum("sri,ic->src", picker_b, drafts, preferred_element_type=jnp.float32)
        .astype(jnp.bfloat16)
        .reshape(tok_group, -1)
    )
    sorted_pos = jnp.sum(jnp.where(picker, row_pos[None, None, :], 0), axis=2).reshape(-1)
    sorted_seq = jnp.repeat(jnp.arange(SEQ_DP), STEPS)
    max_parts, sum_parts, acc_parts = ([], [], [])
    for seq_idx in range(SEQ_DP):
        live_len = lengths[seq_idx] - shard_start
        query_rows = sorted_q[seq_idx].reshape(STEPS * head_count, -1)
        run_max, run_sum, weighted = scan_cache(
            query_rows, cache[seq_idx], live_len, block_len, block_total
        )
        max_parts.append(run_max.reshape(STEPS, head_count))
        sum_parts.append(run_sum.reshape(STEPS, head_count))
        acc_parts.append(weighted.reshape(STEPS, head_count, LAT))
    local_max = jnp.concatenate(max_parts, axis=0)
    local_sum = jnp.concatenate(sum_parts, axis=0)
    local_acc = jnp.concatenate(acc_parts, axis=0)
    recv_acc, recv_max, recv_sum = (
        lax.all_to_all(local_acc[None], "kv", split_axis=2, concat_axis=0, tiled=True),
        lax.all_to_all(local_max[None], "kv", split_axis=2, concat_axis=0, tiled=True),
        lax.all_to_all(local_sum[None], "kv", split_axis=2, concat_axis=0, tiled=True),
    )
    head_max = jnp.max(recv_max, axis=0)
    rescale = jnp.exp(recv_max - head_max[None])
    head_acc = jnp.sum(recv_acc * rescale[..., None], axis=0)
    head_sum = jnp.sum(recv_sum * rescale, axis=0)
    head_q = lax.dynamic_slice_in_dim(
        sorted_q.reshape(tok_group, head_count, -1), kv_index * head_local, head_local, 1
    )
    draft_scores = (
        jnp.einsum("thc,jc->thj", head_q, sorted_drafts, preferred_element_type=jnp.float32)
        * qk_scale
    )
    draft_valid = (sorted_seq[:, None] == sorted_seq[None, :]) & (
        sorted_pos[None, :] <= sorted_pos[:, None]
    )
    draft_scores = jnp.where(draft_valid[:, None, :], draft_scores, -1e30)
    final_max = jnp.maximum(head_max, jnp.max(draft_scores, axis=2))
    adjust = jnp.exp(head_max - final_max)
    draft_weight = jnp.where(
        draft_valid[:, None, :], jnp.exp(draft_scores - final_max[:, :, None]), 0.0
    )
    denom = head_sum * adjust + jnp.sum(draft_weight, axis=2)
    numer = head_acc * adjust[:, :, None] + jnp.einsum(
        "thj,jl->thl",
        draft_weight.astype(jnp.bfloat16),
        sorted_drafts[:, :LAT],
        preferred_element_type=jnp.float32,
    )
    latent_sorted = (
        (numer / denom[:, :, None]).astype(jnp.bfloat16).reshape(SEQ_DP, STEPS, head_local, LAT)
    )
    latent_rows = jnp.einsum(
        "sri,srhl->ihl", picker_b, latent_sorted, preferred_element_type=jnp.float32
    ).astype(jnp.bfloat16)
    all_latents = lax.all_gather(latent_rows, "dp", axis=0, tiled=True)
    all_values = jnp.einsum(
        "thl,hlv->thv", all_latents, w_uv, preferred_element_type=jnp.float32
    ).astype(jnp.bfloat16)
    row_total = all_values.shape[0]
    attn_part = jnp.dot(
        all_values.reshape(row_total, head_local * HD), w_out, preferred_element_type=jnp.float32
    )
    attended = lax.psum(attn_part, "kv")
    resid = (hidden.astype(jnp.float32) + attended).astype(jnp.bfloat16)
    resid_f = resid.astype(jnp.float32)
    square_part = jnp.sum(resid_f * resid_f, axis=1)
    scaled = (resid_f * gain[None, :]).astype(jnp.bfloat16)
    gate_part = jnp.dot(scaled, w_gate, preferred_element_type=jnp.float32)
    up_part = jnp.dot(scaled, w_up, preferred_element_type=jnp.float32)
    gate_sum, up_sum, square_sum = lax.psum((gate_part, up_part, square_part), "dp")
    inv_rms = lax.rsqrt(square_sum / D + 1e-06)[:, None]
    act = (jax.nn.silu(gate_sum * inv_rms) * (up_sum * inv_rms)).astype(jnp.bfloat16)
    down_part = jnp.dot(act, w_down, preferred_element_type=jnp.float32)
    down_sum = lax.psum(down_part, "kv")
    return (resid_f + down_sum).astype(jnp.bfloat16)


CHUNK = 1024
MASKED = -1e30
F32 = jnp.float32
BF16 = jnp.bfloat16
SPEC_VMEM = pl.BlockSpec(memory_space=pltpu.VMEM)
SPEC_SMEM = pl.BlockSpec(memory_space=pltpu.SMEM)
SPEC_ANY = pl.BlockSpec(memory_space=pl.ANY)
MIB = 1024 * 1024


def dot_f32(lhs, rhs, contract=((1,), (0,))):
    return lax.dot_general(lhs, rhs, (contract, ((), ())), preferred_element_type=F32)


def held(array):
    return pltpu.with_memory_space_constraint(array, pltpu.VMEM)


def in_hbm(array):
    return pltpu.with_memory_space_constraint(array, pltpu.HBM)


def three_terms(exact):
    high = exact.astype(BF16).astype(F32)
    middle = (exact - high).astype(BF16).astype(F32)
    low = (exact - high - middle).astype(BF16).astype(F32)
    return high, middle, low


def pack_logs(logs):
    spread = jnp.concatenate(three_terms(logs) + (jnp.zeros_like(logs),), axis=1)
    return jnp.concatenate([spread, jnp.zeros_like(spread)], axis=0).astype(BF16)


def unpack_logs(spread, rows_in):
    spread = spread.astype(F32)[:rows_in, :]
    return spread[:, :128] + spread[:, 128:256] + spread[:, 256:384]


def attention_kernel(
    kv_count, weight_count, len_ref, seq_ref, pos_ref, draft_ref, query_hbm, key_hbm, *rest
):
    weights_hbm = rest[:weight_count]
    mine_ref, theirs_ref = rest[weight_count : weight_count + 2]
    weights_ref = rest[weight_count + 2 : 2 * weight_count + 2]
    (query_t, keys, query_s, acc, row_max, row_sum, logs, query_sem, key_sem, weight_sem) = rest[
        2 * weight_count + 2 :
    ]
    rows_in, width, head_count = query_hbm.shape
    seqs, _, ctx = key_hbm.shape
    steps = rows_in // seqs
    head_local = head_count // kv_count
    lat = acc.shape[1]
    pair = 2 * CHUNK
    pair_total = ctx // pair
    factor = (HD + ROPE) ** (-0.5) * 1.4426950408889634
    me = lax.axis_index("kv")
    core = lax.rem(me, 2)

    row_of = []
    for s in range(seqs):
        found = jnp.int32(0)
        slots = [jnp.int32(0)] * steps
        for r in range(rows_in):
            mine = seq_ref[r] == s
            slots = [jnp.where(mine & (found == i), r, slots[i]) for i in range(steps)]
            found = found + mine.astype(jnp.int32)
        row_of.append(slots)

    def key_copy(s, c):
        cols = pl.ds(pl.multiple_of(c * CHUNK, CHUNK), CHUNK)
        return pltpu.make_async_copy(key_hbm.at[s, :, cols], keys.at[s, :, cols], key_sem.at[s, c])

    def query_copy(s, i):
        return pltpu.make_async_copy(
            query_hbm.at[row_of[s][i]], query_t.at[s * steps + i], query_sem.at[s, i]
        )

    for i in range(steps):
        query_copy(0, i).start()
    later_copies = [key_copy(s, c) for s in range(seqs) for c in range(2 * pair_total)]
    later_copies.pop(0).start()
    later_copies += [query_copy(s, i) for s in range(1, seqs) for i in range(steps)]
    weight_copies = [
        pltpu.make_async_copy(weights_hbm[w], weights_ref[w], weight_sem.at[w]) for w in range(weight_count)
    ]

    def turn_queries(s, meanwhile=()):
        for i in range(steps):
            query_copy(s, i).wait()
        for copy in meanwhile:
            copy.start()
        for i in range(steps):
            query_s[s, i * head_count : (i + 1) * head_count, :] = query_t[s * steps + i].T

    turn_queries(0, later_copies[:1])
    for copy in later_copies[1:]:
        copy.start()
    weight_start = [(0, pair_total - 1) if w < 2 else (seqs - 1, 0) for w in range(weight_count)]

    row_iota = lax.broadcasted_iota(jnp.int32, (rows_in, 128), 0)
    owner = me == kv_count - 1
    logs[...] = jnp.zeros_like(logs)

    for s in range(seqs):
        if s > 0:
            turn_queries(s)

        @pl.when(jnp.logical_not(owner))
        def start_empty():
            row_max[...] = jnp.full_like(row_max, MASKED)
            row_sum[...] = jnp.zeros_like(row_sum)
            acc[...] = jnp.zeros_like(acc)

        @pl.when(owner)
        def start_drafts():
            draft_pad = jnp.concatenate(
                [draft_ref[...].astype(F32), jnp.zeros((128 - rows_in, width), F32)], axis=0
            ).astype(BF16)
            lane = lax.broadcasted_iota(jnp.int32, (1, 128), 1)
            score = dot_f32(query_s[s], draft_pad, ((1,), (1,)))
            masks = []
            for i in range(steps):
                admitted = jnp.zeros((1, 128), jnp.int32)
                for r in range(rows_in):
                    fits = (seq_ref[r] == s) & (pos_ref[r] <= pos_ref[row_of[s][i]])
                    admitted = jnp.where(lane == r, fits.astype(jnp.int32), admitted)
                masks.append(jnp.broadcast_to(admitted, (head_count, 128)))
            mask = jnp.concatenate(masks, axis=0) > 0
            score = jnp.where(mask, score, MASKED)
            first_max = jnp.broadcast_to(jnp.max(score, axis=1, keepdims=True), score.shape)
            weight = jnp.where(mask, jnp.exp2((score - first_max) * factor), 0.0)
            row_max[...] = first_max
            row_sum[...] = weight
            acc[...] = dot_f32(weight.astype(BF16), draft_pad[:, :lat])

        live = jnp.clip(len_ref[s] - me * ctx, 0, ctx)
        live_pairs = lax.div(live + (pair - 1), pair)

        def add_pair_of_chunks(base, masked):
            halves = [pl.ds(base, CHUNK), pl.ds(base + CHUNK, CHUNK)]
            scores = []
            for h in range(2):
                key_copy(s, lax.div(base, CHUNK) + h).wait()
                scores.append(dot_f32(query_s[s], keys[s, :, halves[h]]))
            for h in range(2):
                score = scores[h]
                if masked:
                    place = base + h * CHUNK + lax.broadcasted_iota(jnp.int32, (1, CHUNK), 1)
                    score = jnp.where(place < live, score, MASKED)
                old_max = row_max[...]
                new_max = jnp.maximum(old_max, jnp.max(score, axis=1, keepdims=True))
                scale = jnp.exp2((old_max - new_max) * factor)
                weight = jnp.exp2((score - jnp.concatenate([new_max] * (CHUNK // 128), axis=1)) * factor)
                part = weight[:, :128]
                for c in range(1, CHUNK // 128):
                    part = part + weight[:, c * 128 : (c + 1) * 128]
                row_max[...] = new_max
                row_sum[...] = row_sum[...] * scale + part
                update = dot_f32(weight.astype(BF16), keys[s, :lat, halves[h]], ((1,), (1,)))
                acc[...] = acc[...] * jnp.concatenate([scale] * (lat // 128), axis=1) + update

        def visit(j, carry):
            for copy, (at_seq, at_block) in zip(weight_copies, weight_start):
                if at_seq == s:
                    @pl.when(j == at_block)
                    def start_weight(copy=copy):
                        copy.start()
            base = pl.multiple_of(j * pair, pair)
            whole = base + pair <= live

            @pl.when(whole)
            def all_live():
                add_pair_of_chunks(base, False)

            @pl.when(jnp.logical_not(whole))
            def some_live():
                add_pair_of_chunks(base, True)

            return carry

        lax.fori_loop(0, live_pairs, visit, 0)

        def skip(j, carry):
            key_copy(s, 2 * j).wait()
            key_copy(s, 2 * j + 1).wait()
            return carry

        lax.fori_loop(live_pairs, pair_total, skip, 0)
        for copy, (at_seq, at_block) in zip(weight_copies, weight_start):
            if at_seq == s:
                @pl.when(live_pairs <= at_block)
                def start_weight(copy=copy):
                    copy.start()

        total = jnp.sum(row_sum[...], axis=1, keepdims=True)
        some = total > 0.0
        acc[...] = acc[...] * jnp.where(some, 1.0 / jnp.where(some, total, 1.0), 0.0)
        log_sum = jnp.where(
            some, row_max[...] * factor + jnp.log2(jnp.where(some, total, 1.0)), MASKED
        )
        for i in range(steps):
            flat = log_sum[i * head_count : (i + 1) * head_count, :].T[:1, :]
            logs[...] = jnp.where(row_iota == row_of[s][i], flat, logs[...])
            for b in range(kv_count // 2):
                base = (b * rows_in + row_of[s][i]) * head_local
                target = pl.ds(pl.multiple_of(base, head_local), head_local)
                for ref, side in ((mine_ref, core), (theirs_ref, 1 - core)):
                    start = i * head_count + (2 * b + side) * head_local
                    source = pl.ds(pl.multiple_of(start, head_local), head_local)
                    ref[target, :] = acc[source, :].astype(BF16)

    spread = pack_logs(logs[...])
    body = rows_in * head_count // 2
    mine_ref[body:, :] = spread
    theirs_ref[body:, :] = spread
    for copy in weight_copies:
        copy.wait()


def attention(kv_count, lengths, row_seq, row_pos, drafts, query_t, key_t, weights):
    rows_in, width, head_count = query_t.shape
    seqs, _, ctx = key_t.shape
    group = rows_in // seqs * head_count
    message = pltpu.VMEM((rows_in * head_count // 2 + 16, LAT), BF16)
    return pl.pallas_call(
        functools.partial(attention_kernel, kv_count, len(weights)),
        out_shape=[message] * 2 + [pltpu.VMEM(weight.shape, weight.dtype) for weight in weights],
        in_specs=[SPEC_SMEM] * 3 + [SPEC_VMEM] + [SPEC_ANY] * (2 + len(weights)),
        out_specs=[SPEC_VMEM] * 2 + [SPEC_ANY] * len(weights),
        scratch_shapes=[
            pltpu.VMEM(query_t.shape, BF16),
            pltpu.VMEM(key_t.shape, BF16),
            pltpu.VMEM((seqs, group, width), BF16),
            pltpu.VMEM((group, LAT), F32),
            pltpu.VMEM((group, 128), F32),
            pltpu.VMEM((group, 128), F32),
            pltpu.VMEM((rows_in, 128), F32),
            pltpu.SemaphoreType.DMA((seqs, rows_in // seqs)),
            pltpu.SemaphoreType.DMA((seqs, ctx // CHUNK)),
            pltpu.SemaphoreType.DMA((len(weights),)),
        ],
        compiler_params=pltpu.CompilerParams(vmem_limit_bytes=26 * MIB),
        cost_estimate=pl.CostEstimate(
            flops=2 * seqs * group * ctx * (width + LAT),
            bytes_accessed=2 * seqs * ctx * width,
            transcendentals=seqs * group * ctx,
        ),
        name="attention",
    )(*[in_hbm(arg) for arg in (lengths, row_seq, row_pos, drafts, query_t, key_t, *weights)])


def merge_shares(logs):
    peak = functools.reduce(jnp.maximum, logs)
    shares = [jnp.exp2(log - peak) for log in logs]
    total = functools.reduce(jnp.add, shares)
    shares = [share / total for share in shares]
    rows = sum(share.shape[0] for share in shares)
    stacked = jnp.concatenate(shares + [jnp.zeros((128 - rows, 128), F32)], axis=0)
    return stacked.T, peak + jnp.log2(total)


def merge_pair_kernel(rows_in, heads, mine_ref, sibling_ref, *rest):
    outs, mix = rest[:-1], rest[-1]
    blocks = len(outs)
    body = blocks * rows_in * heads
    me = lax.axis_index("kv")
    chip, core = lax.div(me, 2), lax.rem(me, 2)
    parts = (mine_ref, sibling_ref)
    mix[...], log_sum = merge_shares([unpack_logs(part[body:, :], rows_in) for part in parts])
    spread = pack_logs(log_sum)
    for k in range(blocks):
        block = jnp.bitwise_xor(chip, k)
        share = mix[pl.ds(pl.multiple_of((2 * block + core) * heads, heads), heads), :]
        for r in range(rows_in):
            source = pl.ds(pl.multiple_of((block * rows_in + r) * heads, heads), heads)
            whole = jnp.zeros((heads, LAT), F32)
            for p in range(2):
                at = p * rows_in + r
                whole = whole + parts[p][source, :].astype(F32) * share[:, at : at + 1]
            outs[k][r * heads : (r + 1) * heads, :] = whole.astype(BF16)
        outs[k][rows_in * heads :, :] = spread


def merge_pair(rows_in, heads, mine, sibling):
    blocks = (mine.shape[0] - 16) // (rows_in * heads)
    message = jax.ShapeDtypeStruct((rows_in * heads + 16, LAT), BF16)
    return pl.pallas_call(
        functools.partial(merge_pair_kernel, rows_in, heads),
        out_shape=[message] * blocks,
        in_specs=[SPEC_VMEM] * 2,
        out_specs=[SPEC_VMEM] * blocks,
        scratch_shapes=[pltpu.VMEM((128, 128), F32)],
        compiler_params=pltpu.CompilerParams(vmem_limit_bytes=8 * MIB),
        name="merge_pair",
    )(mine, sibling)


def merge_values_kernel(rows_in, w_ref, *rest):
    parts = rest[:-3]
    out_ref, mix, latent = rest[-3:]
    heads = w_ref.shape[0]
    body = rows_in * heads
    me = lax.axis_index("kv")
    mix[...], _ = merge_shares([unpack_logs(part[body:, :], rows_in) for part in parts])
    share = mix[pl.ds(pl.multiple_of(me * heads, heads), heads), :]
    for r in range(rows_in):
        block = slice(r * heads, (r + 1) * heads)
        whole = jnp.zeros((heads, LAT), F32)
        for k, part in enumerate(parts):
            at = k * rows_in + r
            whole = whole + part[block, :].astype(F32) * share[:, at : at + 1]
        for c in range(LAT // 128):
            latent[c, block, :] = whole[:, c * 128 : (c + 1) * 128]
    for h in range(heads):
        pieces = [latent[c, pl.ds(h, rows_in, stride=heads), :] for c in range(LAT // 128)]
        rows = jnp.concatenate(pieces, axis=1).astype(BF16)
        out_ref[:, h * HD : (h + 1) * HD] = dot_f32(rows, w_ref[h]).astype(BF16)


def merge_values(rows_in, w_uv, parts):
    heads = w_uv.shape[0]
    return pl.pallas_call(
        functools.partial(merge_values_kernel, rows_in),
        out_shape=jax.ShapeDtypeStruct((rows_in, heads * HD), BF16),
        in_specs=[SPEC_VMEM] * (1 + len(parts)),
        out_specs=SPEC_VMEM,
        scratch_shapes=[pltpu.VMEM((128, 128), F32), pltpu.VMEM((LAT // 128, rows_in * heads, 128), F32)],
        compiler_params=pltpu.CompilerParams(vmem_limit_bytes=8 * MIB),
        name="merge_values",
    )(held(w_uv), *parts)


def core_span(side, half):
    core = lax.rem(lax.axis_index("kv"), 2)
    return pl.ds(pl.multiple_of((core if side == 0 else 1 - core) * half, half), half)


def project_theirs_kernel(flips, w_ref, *rest):
    parts = rest[:-3]
    rows_ref, theirs_ref, whole = rest[-3:]
    rows = parts[0].shape[0]
    at = lax.axis_index("dp")
    for k, part in zip(flips, parts):
        place = pl.ds(pl.multiple_of(jnp.bitwise_xor(at, k) * rows, rows), rows)
        whole[place, :] = part[...].astype(F32)
    stacked = whole[...].astype(BF16)
    rows_ref[...] = stacked
    theirs_ref[...] = dot_f32(stacked, w_ref[:, core_span(1, theirs_ref.shape[1])]).astype(BF16)


def project_mine_kernel(w_ref, rows_ref, mine_ref):
    mine_ref[...] = dot_f32(rows_ref[...], w_ref[:, core_span(0, mine_ref.shape[1])])


def project(weight, parts, flips, name):
    rows, depth = parts[0].shape
    rows = rows * len(parts)
    half = weight.shape[1] // 2
    params = pltpu.CompilerParams(vmem_limit_bytes=8 * MIB)
    cost = pl.CostEstimate(
        flops=2 * rows * depth * half, bytes_accessed=2 * depth * half, transcendentals=0
    )
    stacked, theirs = pl.pallas_call(
        functools.partial(project_theirs_kernel, flips),
        out_shape=[jax.ShapeDtypeStruct((rows, depth), BF16), jax.ShapeDtypeStruct((rows, half), BF16)],
        in_specs=[SPEC_VMEM] * (1 + len(parts)),
        out_specs=[SPEC_VMEM] * 2,
        scratch_shapes=[pltpu.VMEM((rows, depth), F32)],
        compiler_params=params,
        cost_estimate=cost,
        name=name + "_theirs",
    )(held(weight), *parts)
    mine = pl.pallas_call(
        project_mine_kernel,
        out_shape=jax.ShapeDtypeStruct((rows, half), F32),
        in_specs=[SPEC_VMEM] * 2,
        out_specs=SPEC_VMEM,
        compiler_params=params,
        cost_estimate=cost,
        name=name + "_mine",
    )(held(weight), stacked)
    return mine, theirs


def add_pair_kernel(mine_ref, sibling_ref, out_ref):
    out_ref[...] = (mine_ref[...] + sibling_ref[...].astype(F32)).astype(BF16)


def add_pair(mine, sibling):
    return pl.pallas_call(
        add_pair_kernel,
        out_shape=jax.ShapeDtypeStruct(mine.shape, BF16),
        in_specs=[SPEC_VMEM] * 2,
        out_specs=SPEC_VMEM,
        compiler_params=pltpu.CompilerParams(vmem_limit_bytes=4 * MIB),
        name="add_pair",
    )(mine, sibling)


def add_tree(parts):
    parts = [part[...].astype(F32) for part in parts]
    while len(parts) > 1:
        parts = [parts[i] + parts[i + 1] for i in range(0, len(parts), 2)]
    return parts[0]


def add_chips_kernel(base_ref, *rest):
    parts, out_ref = rest[:-1], rest[-1]
    half = out_ref.shape[1]
    base = base_ref[...]
    if base.shape[1] > half:
        core = lax.rem(lax.axis_index("kv"), 2)
        base = jnp.where(core == 0, base[:, :half].astype(F32), base[:, half:].astype(F32))
    out_ref[...] = (base.astype(F32) + add_tree(parts)).astype(BF16)


def add_chips(base, parts, name):
    return pl.pallas_call(
        add_chips_kernel,
        out_shape=jax.ShapeDtypeStruct(parts[0].shape, BF16),
        in_specs=[SPEC_VMEM] * (1 + len(parts)),
        out_specs=SPEC_VMEM,
        compiler_params=pltpu.CompilerParams(vmem_limit_bytes=4 * MIB),
        name=name,
    )(base, *parts)


def expand_half(side, gate_ref, up_ref, gain_ref, resid):
    half = resid.shape[1]
    span = core_span(side, half)
    scaled = (resid * gain_ref[:, span]).astype(BF16)
    square = jnp.sum(resid * resid, axis=1, keepdims=True)
    return dot_f32(scaled, gate_ref[span, :]), dot_f32(scaled, up_ref[span, :]), square


def expand_mine_kernel(gate_ref, up_ref, gain_ref, mine_ref, sums_ref, square_ref):
    width = gate_ref.shape[1]
    gate, up, square = expand_half(0, gate_ref, up_ref, gain_ref, mine_ref[...].astype(F32))
    sums_ref[:, :width] = gate
    sums_ref[:, width:] = up
    square_ref[...] = jnp.broadcast_to(square, square_ref.shape)


def expand_rest_kernel(gate_ref, up_ref, gain_ref, sibling_ref, sums_ref, square_ref, *rest):
    outs, total = rest[:-1], rest[-1]
    rows = outs[0].shape[0]
    width = gate_ref.shape[1]
    at = lax.axis_index("dp")
    gate, up, square = expand_half(1, gate_ref, up_ref, gain_ref, sibling_ref[...].astype(F32))
    total[:, :width] = sums_ref[:, :width] + gate
    total[:, width : 2 * width] = sums_ref[:, width:] + up
    lane = lax.broadcasted_iota(jnp.int32, square_ref.shape, 1)
    terms = three_terms(square_ref[...] + square)
    tail = jnp.zeros(lane.shape, F32)
    for t in range(3):
        tail = jnp.where(lane == t, terms[t], tail)
    total[:, 2 * width :] = tail
    for k in range(len(outs)):
        place = pl.ds(pl.multiple_of(jnp.bitwise_xor(at, k) * rows, rows), rows)
        outs[k][...] = total[place, :].astype(BF16)


def expand(dp_count, w_gate, w_up, gain, mine, sibling):
    cols, width = w_gate.shape
    rows = mine.shape[0]
    params = pltpu.CompilerParams(vmem_limit_bytes=8 * MIB)
    cost = pl.CostEstimate(
        flops=2 * rows * cols * width, bytes_accessed=2 * cols * width, transcendentals=0
    )
    weights = (held(w_gate), held(w_up), gain.reshape(1, cols))
    sums, square = pl.pallas_call(
        expand_mine_kernel,
        out_shape=[
            jax.ShapeDtypeStruct((rows, 2 * width), F32),
            jax.ShapeDtypeStruct((rows, 128), F32),
        ],
        in_specs=[SPEC_VMEM] * 4,
        out_specs=[SPEC_VMEM] * 2,
        compiler_params=params,
        cost_estimate=cost,
        name="gate_up_mine",
    )(*weights, mine)
    message = jax.ShapeDtypeStruct((rows // dp_count, 2 * width + 128), BF16)
    return pl.pallas_call(
        expand_rest_kernel,
        out_shape=[message] * dp_count,
        in_specs=[SPEC_VMEM] * 6,
        out_specs=[SPEC_VMEM] * dp_count,
        scratch_shapes=[pltpu.VMEM((rows, 2 * width + 128), F32)],
        compiler_params=params,
        cost_estimate=cost,
        name="gate_up_rest",
    )(*weights, sibling, sums, square)


def activate_kernel(*rest):
    parts, out_ref = rest[:-1], rest[-1]
    width = out_ref.shape[1]
    total = functools.reduce(jnp.add, [part[...].astype(F32) for part in parts])
    square = jnp.sum(total[:, 2 * width :], axis=1, keepdims=True)
    inv_rms = lax.rsqrt(square / D + 1e-06)
    gate = total[:, :width] * inv_rms
    up = total[:, width : 2 * width] * inv_rms
    out_ref[...] = (gate / (1.0 + jnp.exp(-gate)) * up).astype(BF16)


def activate(parts):
    rows, wide = parts[0].shape
    return pl.pallas_call(
        activate_kernel,
        out_shape=jax.ShapeDtypeStruct((rows, (wide - 128) // 2), BF16),
        in_specs=[SPEC_VMEM] * len(parts),
        out_specs=SPEC_VMEM,
        compiler_params=pltpu.CompilerParams(vmem_limit_bytes=4 * MIB),
        name="activate",
    )(*parts)


def assemble_kernel(mine_ref, sibling_ref, out_ref):
    half = mine_ref.shape[1]
    left = lax.rem(lax.axis_index("kv"), 2) == 0
    mine, sibling = mine_ref[...].astype(F32), sibling_ref[...].astype(F32)
    out_ref[:, :half] = jnp.where(left, mine, sibling).astype(BF16)
    out_ref[:, half:] = jnp.where(left, sibling, mine).astype(BF16)


def assemble(mine, sibling):
    rows, half = mine.shape
    return pl.pallas_call(
        assemble_kernel,
        out_shape=jax.ShapeDtypeStruct((rows, 2 * half), BF16),
        in_specs=[SPEC_VMEM] * 2,
        out_specs=SPEC_VMEM,
        compiler_params=pltpu.CompilerParams(vmem_limit_bytes=4 * MIB),
        name="assemble",
    )(mine, sibling)


def partner(array, axis, flip):
    pairs = [(i, i ^ flip) for i in range(lax.axis_size(axis))]
    return lax.ppermute(array, axis, pairs)


def swap(parts, axis, unit, flips):
    return [partner(parts[k], axis, k * unit) if k else parts[0] for k in flips]


def line_flips(count):
    return [*range(2, count), 1, 0]


def grid_flips(count):
    return list(range(count - 1, -1, -1))


def sum_over_kv(weight, parts, flips, base, name):
    chips = lax.axis_size("kv") // 2
    mine, theirs = project(weight, parts, flips, name)
    pair = add_pair(mine, partner(theirs, "kv", 1))
    half = add_chips(base, swap([pair] * chips, "kv", 2, range(chips)), name + "_sum")
    return half, partner(half, "kv", 1)


def on_device_tiled(
    queries, drafts, cache, lengths, row_seq, row_pos, w_uv, w_out, hidden, gain, w_gate, w_up, w_down
):
    kv_count = lax.axis_size("kv")
    dp_count = lax.axis_size("dp")
    rows_in, head_count = queries.shape[:2]
    flips = line_flips(dp_count)
    query_t = jnp.swapaxes(queries, 1, 2)
    key_t = jnp.swapaxes(cache, 1, 2)
    mine, theirs, w_uv, w_out, w_gate, w_up = attention(
        kv_count, lengths, row_seq, row_pos, drafts, query_t, key_t, [w_uv, w_out, w_gate, w_up]
    )
    blocks = merge_pair(rows_in, head_count // kv_count, mine, partner(theirs, "kv", 1))
    values = merge_values(rows_in, w_uv, swap(blocks, "kv", 2, grid_flips(len(blocks))))
    resid, resid_sibling = sum_over_kv(w_out, swap([values] * dp_count, "dp", 1, flips), flips, hidden, "project_out")
    sums = expand(dp_count, w_gate, w_up, gain, resid, resid_sibling)
    act = activate(swap(sums, "dp", 1, flips))
    mixed, mixed_sibling = sum_over_kv(w_down, swap([act] * dp_count, "dp", 1, flips), flips, resid, "project_down")
    return assemble(mixed, mixed_sibling)


def tiles_fit(kv_count, dp_count, head_count, rows_in, cols, ctx):
    powers = kv_count & (kv_count - 1) == 0 and dp_count & (dp_count - 1) == 0
    heads = head_count % (16 * kv_count) == 0 and head_count == 128 and kv_count * rows_in <= 128
    return powers and heads and rows_in == 8 and cols % 256 == 0 and ctx % (2 * CHUNK) == 0


def solution(mesh):
    placed = (
        P("dp", None, None),
        P("dp", None),
        P("dp", "kv", None),
        P("dp"),
        P("dp"),
        P("dp"),
        P("kv", None, None),
        P("kv", "dp"),
        P(None, "dp"),
        P("dp"),
        P("dp", "kv"),
        P("dp", "kv"),
        P("kv", "dp"),
    )

    def placed_call(body):
        return jax.shard_map(
            body, mesh=mesh, in_specs=placed, out_specs=P(None, "dp"), check_vma=False
        )

    def run(*args):
        kv_count, dp_count = mesh.shape["kv"], mesh.shape["dp"]
        queries, cache, hidden = args[0], args[2], args[8]
        fits = tiles_fit(
            kv_count,
            dp_count,
            queries.shape[1],
            queries.shape[0] // dp_count,
            hidden.shape[1] // dp_count,
            cache.shape[1] // kv_count,
        )
        return placed_call(on_device_tiled if fits else on_device)(*args)

    return run
```

```python
import functools

import jax
import jax.numpy as jnp
from jax import lax
from jax.experimental import pallas as pl
from jax.experimental.pallas import tpu as pltpu
from jax.sharding import PartitionSpec as P

D = 7168
LAT = 512
ROPE = 64
HD = 128
SEQ_DP = 2
STEPS = 4


def scan_cache(query_rows, key_rows, live_len, block_len, block_count):
    qk_scale = (HD + ROPE) ** (-0.5)
    row_count = query_rows.shape[0]

    def visit(block_idx, carry):
        run_max, run_sum, weighted = carry
        key_block = lax.dynamic_slice_in_dim(key_rows, block_idx * block_len, block_len, 0)
        scores = (
            jnp.einsum("rc,kc->rk", query_rows, key_block, preferred_element_type=jnp.float32)
            * qk_scale
        )
        valid = block_idx * block_len + jnp.arange(block_len) < live_len
        scores = jnp.where(valid[None, :], scores, -1e30)
        new_max = jnp.maximum(run_max, jnp.max(scores, axis=1))
        weights = jnp.where(valid[None, :], jnp.exp(scores - new_max[:, None]), 0.0)
        factor = jnp.exp(run_max - new_max)
        run_sum = run_sum * factor + jnp.sum(weights, axis=1)
        weighted = weighted * factor[:, None] + jnp.dot(
            weights.astype(jnp.bfloat16), key_block[:, :LAT], preferred_element_type=jnp.float32
        )
        return (new_max, run_sum, weighted)

    start_carry = (
        jnp.full((row_count,), -1e30, jnp.float32),
        jnp.zeros((row_count,), jnp.float32),
        jnp.zeros((row_count, LAT), jnp.float32),
    )
    return lax.fori_loop(0, block_count, visit, start_carry)


def on_device(
    queries,
    drafts,
    cache,
    lengths,
    row_seq,
    row_pos,
    w_uv,
    w_out,
    hidden,
    gain,
    w_gate,
    w_up,
    w_down,
):
    kv_count = lax.axis_size("kv")
    kv_index = lax.axis_index("kv")
    tok_group, head_count = (queries.shape[0], queries.shape[1])
    head_local = head_count // kv_count
    ctx_dev = cache.shape[1]
    shard_start = kv_index * ctx_dev
    block_len = min(512, ctx_dev)
    block_total = ctx_dev // block_len
    qk_scale = (HD + ROPE) ** (-0.5)
    order_idx = jnp.arange(tok_group)
    same_seq = row_seq[:, None] == row_seq[None, :]
    rank_in_seq = jnp.sum(same_seq & (order_idx[:, None] > order_idx[None, :]), axis=1)
    picker = (row_seq[None, None, :] == jnp.arange(SEQ_DP)[:, None, None]) & (
        rank_in_seq[None, None, :] == jnp.arange(STEPS)[None, :, None]
    )
    picker_b = picker.astype(jnp.bfloat16)
    sorted_q = jnp.einsum(
        "sri,ihc->srhc", picker_b, queries, preferred_element_type=jnp.float32
    ).astype(jnp.bfloat16)
    sorted_drafts = (
        jnp.einsum("sri,ic->src", picker_b, drafts, preferred_element_type=jnp.float32)
        .astype(jnp.bfloat16)
        .reshape(tok_group, -1)
    )
    sorted_pos = jnp.sum(jnp.where(picker, row_pos[None, None, :], 0), axis=2).reshape(-1)
    sorted_seq = jnp.repeat(jnp.arange(SEQ_DP), STEPS)
    max_parts, sum_parts, acc_parts = ([], [], [])
    for seq_idx in range(SEQ_DP):
        live_len = lengths[seq_idx] - shard_start
        query_rows = sorted_q[seq_idx].reshape(STEPS * head_count, -1)
        run_max, run_sum, weighted = scan_cache(
            query_rows, cache[seq_idx], live_len, block_len, block_total
        )
        max_parts.append(run_max.reshape(STEPS, head_count))
        sum_parts.append(run_sum.reshape(STEPS, head_count))
        acc_parts.append(weighted.reshape(STEPS, head_count, LAT))
    local_max = jnp.concatenate(max_parts, axis=0)
    local_sum = jnp.concatenate(sum_parts, axis=0)
    local_acc = jnp.concatenate(acc_parts, axis=0)
    recv_acc, recv_max, recv_sum = (
        lax.all_to_all(local_acc[None], "kv", split_axis=2, concat_axis=0, tiled=True),
        lax.all_to_all(local_max[None], "kv", split_axis=2, concat_axis=0, tiled=True),
        lax.all_to_all(local_sum[None], "kv", split_axis=2, concat_axis=0, tiled=True),
    )
    head_max = jnp.max(recv_max, axis=0)
    rescale = jnp.exp(recv_max - head_max[None])
    head_acc = jnp.sum(recv_acc * rescale[..., None], axis=0)
    head_sum = jnp.sum(recv_sum * rescale, axis=0)
    head_q = lax.dynamic_slice_in_dim(
        sorted_q.reshape(tok_group, head_count, -1), kv_index * head_local, head_local, 1
    )
    draft_scores = (
        jnp.einsum("thc,jc->thj", head_q, sorted_drafts, preferred_element_type=jnp.float32)
        * qk_scale
    )
    draft_valid = (sorted_seq[:, None] == sorted_seq[None, :]) & (
        sorted_pos[None, :] <= sorted_pos[:, None]
    )
    draft_scores = jnp.where(draft_valid[:, None, :], draft_scores, -1e30)
    final_max = jnp.maximum(head_max, jnp.max(draft_scores, axis=2))
    adjust = jnp.exp(head_max - final_max)
    draft_weight = jnp.where(
        draft_valid[:, None, :], jnp.exp(draft_scores - final_max[:, :, None]), 0.0
    )
    denom = head_sum * adjust + jnp.sum(draft_weight, axis=2)
    numer = head_acc * adjust[:, :, None] + jnp.einsum(
        "thj,jl->thl",
        draft_weight.astype(jnp.bfloat16),
        sorted_drafts[:, :LAT],
        preferred_element_type=jnp.float32,
    )
    latent_sorted = (
        (numer / denom[:, :, None]).astype(jnp.bfloat16).reshape(SEQ_DP, STEPS, head_local, LAT)
    )
    latent_rows = jnp.einsum(
        "sri,srhl->ihl", picker_b, latent_sorted, preferred_element_type=jnp.float32
    ).astype(jnp.bfloat16)
    all_latents = lax.all_gather(latent_rows, "dp", axis=0, tiled=True)
    all_values = jnp.einsum(
        "thl,hlv->thv", all_latents, w_uv, preferred_element_type=jnp.float32
    ).astype(jnp.bfloat16)
    row_total = all_values.shape[0]
    attn_part = jnp.dot(
        all_values.reshape(row_total, head_local * HD), w_out, preferred_element_type=jnp.float32
    )
    attended = lax.psum(attn_part, "kv")
    resid = (hidden.astype(jnp.float32) + attended).astype(jnp.bfloat16)
    resid_f = resid.astype(jnp.float32)
    square_part = jnp.sum(resid_f * resid_f, axis=1)
    scaled = (resid_f * gain[None, :]).astype(jnp.bfloat16)
    gate_part = jnp.dot(scaled, w_gate, preferred_element_type=jnp.float32)
    up_part = jnp.dot(scaled, w_up, preferred_element_type=jnp.float32)
    gate_sum, up_sum, square_sum = lax.psum((gate_part, up_part, square_part), "dp")
    inv_rms = lax.rsqrt(square_sum / D + 1e-06)[:, None]
    act = (jax.nn.silu(gate_sum * inv_rms) * (up_sum * inv_rms)).astype(jnp.bfloat16)
    down_part = jnp.dot(act, w_down, preferred_element_type=jnp.float32)
    down_sum = lax.psum(down_part, "kv")
    return (resid_f + down_sum).astype(jnp.bfloat16)


CHUNK = 1024
MASKED = -1e30
F32 = jnp.float32
BF16 = jnp.bfloat16
SPEC_VMEM = pl.BlockSpec(memory_space=pltpu.VMEM)
SPEC_SMEM = pl.BlockSpec(memory_space=pltpu.SMEM)
SPEC_ANY = pl.BlockSpec(memory_space=pl.ANY)
MIB = 1024 * 1024


def dot_f32(lhs, rhs, contract=((1,), (0,))):
    return lax.dot_general(lhs, rhs, (contract, ((), ())), preferred_element_type=F32)


def held(array):
    return pltpu.with_memory_space_constraint(array, pltpu.VMEM)


def in_hbm(array):
    return pltpu.with_memory_space_constraint(array, pltpu.HBM)


def three_terms(exact):
    high = exact.astype(BF16).astype(F32)
    middle = (exact - high).astype(BF16).astype(F32)
    low = (exact - high - middle).astype(BF16).astype(F32)
    return high, middle, low


def pack_logs(logs):
    spread = jnp.concatenate(three_terms(logs) + (jnp.zeros_like(logs),), axis=1)
    return jnp.concatenate([spread, jnp.zeros_like(spread)], axis=0).astype(BF16)


def unpack_logs(spread, rows_in):
    spread = spread.astype(F32)[:rows_in, :]
    return spread[:, :128] + spread[:, 128:256] + spread[:, 256:384]


def attention_kernel(
    kv_count, weight_count, len_ref, seq_ref, pos_ref, draft_ref, query_hbm, key_hbm, *rest
):
    weights_hbm = rest[:weight_count]
    mine_ref, theirs_ref = rest[weight_count : weight_count + 2]
    weights_ref = rest[weight_count + 2 : 2 * weight_count + 2]
    (query_t, keys, query_s, acc, row_max, row_sum, logs, query_sem, key_sem, weight_sem) = rest[
        2 * weight_count + 2 :
    ]
    rows_in, width, head_count = query_hbm.shape
    seqs, _, ctx = key_hbm.shape
    steps = rows_in // seqs
    head_local = head_count // kv_count
    lat = acc.shape[1]
    pair = 2 * CHUNK
    pair_total = ctx // pair
    factor = (HD + ROPE) ** (-0.5) * 1.4426950408889634
    me = lax.axis_index("kv")
    core = lax.rem(me, 2)

    query_copy = pltpu.make_async_copy(query_hbm, query_t, query_sem)
    query_copy.start()

    def key_copy(s, j):
        cols = pl.ds(pl.multiple_of(j * pair, pair), pair)
        return pltpu.make_async_copy(key_hbm.at[s, :, cols], keys.at[s, :, cols], key_sem.at[s, j])

    later_copies = [key_copy(s, j) for s in range(seqs) for j in range(pair_total)]
    later_copies.pop(0).start()
    weight_copies = [
        pltpu.make_async_copy(weights_hbm[w], weights_ref[w], weight_sem.at[w]) for w in range(weight_count)
    ]

    row_of = []
    for s in range(seqs):
        found = jnp.int32(0)
        slots = [jnp.int32(0)] * steps
        for r in range(rows_in):
            mine = seq_ref[r] == s
            slots = [jnp.where(mine & (found == i), r, slots[i]) for i in range(steps)]
            found = found + mine.astype(jnp.int32)
        row_of.append(slots)

    query_copy.wait()
    for copy in later_copies:
        copy.start()
    for s in range(seqs):
        for i in range(steps):
            query_s[s, i * head_count : (i + 1) * head_count, :] = query_t[row_of[s][i]].T

    row_iota = lax.broadcasted_iota(jnp.int32, (rows_in, 128), 0)
    owner = me == kv_count - 1
    logs[...] = jnp.zeros_like(logs)

    for s in range(seqs):

        @pl.when(jnp.logical_not(owner))
        def start_empty():
            row_max[...] = jnp.full_like(row_max, MASKED)
            row_sum[...] = jnp.zeros_like(row_sum)
            acc[...] = jnp.zeros_like(acc)

        @pl.when(owner)
        def start_drafts():
            draft_pad = jnp.concatenate(
                [draft_ref[...].astype(F32), jnp.zeros((128 - rows_in, width), F32)], axis=0
            ).astype(BF16)
            lane = lax.broadcasted_iota(jnp.int32, (1, 128), 1)
            score = dot_f32(query_s[s], draft_pad, ((1,), (1,)))
            masks = []
            for i in range(steps):
                admitted = jnp.zeros((1, 128), jnp.int32)
                for r in range(rows_in):
                    fits = (seq_ref[r] == s) & (pos_ref[r] <= pos_ref[row_of[s][i]])
                    admitted = jnp.where(lane == r, fits.astype(jnp.int32), admitted)
                masks.append(jnp.broadcast_to(admitted, (head_count, 128)))
            mask = jnp.concatenate(masks, axis=0) > 0
            score = jnp.where(mask, score, MASKED)
            first_max = jnp.broadcast_to(jnp.max(score, axis=1, keepdims=True), score.shape)
            weight = jnp.where(mask, jnp.exp2((score - first_max) * factor), 0.0)
            row_max[...] = first_max
            row_sum[...] = weight
            acc[...] = dot_f32(weight.astype(BF16), draft_pad[:, :lat])

        live = jnp.clip(len_ref[s] - me * ctx, 0, ctx)
        live_pairs = lax.div(live + (pair - 1), pair)

        def add_block(base, masked):
            halves = [pl.ds(base, CHUNK), pl.ds(base + CHUNK, CHUNK)]
            scores = [dot_f32(query_s[s], keys[s, :, half]) for half in halves]
            for h in range(2):
                score = scores[h]
                if masked:
                    place = base + h * CHUNK + lax.broadcasted_iota(jnp.int32, (1, CHUNK), 1)
                    score = jnp.where(place < live, score, MASKED)
                old_max = row_max[...]
                new_max = jnp.maximum(old_max, jnp.max(score, axis=1, keepdims=True))
                scale = jnp.exp2((old_max - new_max) * factor)
                weight = jnp.exp2((score - jnp.concatenate([new_max] * (CHUNK // 128), axis=1)) * factor)
                part = weight[:, :128]
                for c in range(1, CHUNK // 128):
                    part = part + weight[:, c * 128 : (c + 1) * 128]
                row_max[...] = new_max
                row_sum[...] = row_sum[...] * scale + part
                update = dot_f32(weight.astype(BF16), keys[s, :lat, halves[h]], ((1,), (1,)))
                acc[...] = acc[...] * jnp.concatenate([scale] * (lat // 128), axis=1) + update

        def visit(j, carry):
            key_copy(s, j).wait()
            if s == 0:
                for w in range(weight_count):
                    @pl.when(j == w % pair_total)
                    def start_weight():
                        weight_copies[w].start()
            base = pl.multiple_of(j * pair, pair)
            whole = base + pair <= live

            @pl.when(whole)
            def all_live():
                add_block(base, False)

            @pl.when(jnp.logical_not(whole))
            def some_live():
                add_block(base, True)

            return carry

        lax.fori_loop(0, live_pairs, visit, 0)

        def skip(j, carry):
            key_copy(s, j).wait()
            return carry

        lax.fori_loop(live_pairs, pair_total, skip, 0)
        if s == 0:
            for w in range(weight_count):
                @pl.when(live_pairs <= w % pair_total)
                def start_weight():
                    weight_copies[w].start()

        total = jnp.sum(row_sum[...], axis=1, keepdims=True)
        some = total > 0.0
        acc[...] = acc[...] * jnp.where(some, 1.0 / jnp.where(some, total, 1.0), 0.0)
        log_sum = jnp.where(
            some, row_max[...] * factor + jnp.log2(jnp.where(some, total, 1.0)), MASKED
        )
        for i in range(steps):
            flat = log_sum[i * head_count : (i + 1) * head_count, :].T[:1, :]
            logs[...] = jnp.where(row_iota == row_of[s][i], flat, logs[...])
            for b in range(kv_count // 2):
                base = (b * rows_in + row_of[s][i]) * head_local
                target = pl.ds(pl.multiple_of(base, head_local), head_local)
                for ref, side in ((mine_ref, core), (theirs_ref, 1 - core)):
                    start = i * head_count + (2 * b + side) * head_local
                    source = pl.ds(pl.multiple_of(start, head_local), head_local)
                    ref[target, :] = acc[source, :].astype(BF16)

    spread = pack_logs(logs[...])
    body = rows_in * head_count // 2
    mine_ref[body:, :] = spread
    theirs_ref[body:, :] = spread
    for copy in weight_copies:
        copy.wait()


def attention(kv_count, lengths, row_seq, row_pos, drafts, query_t, key_t, weights):
    rows_in, width, head_count = query_t.shape
    seqs, _, ctx = key_t.shape
    group = rows_in // seqs * head_count
    message = pltpu.VMEM((rows_in * head_count // 2 + 16, LAT), BF16)
    return pl.pallas_call(
        functools.partial(attention_kernel, kv_count, len(weights)),
        out_shape=[message] * 2 + [pltpu.VMEM(weight.shape, weight.dtype) for weight in weights],
        in_specs=[SPEC_SMEM] * 3 + [SPEC_VMEM] + [SPEC_ANY] * (2 + len(weights)),
        out_specs=[SPEC_VMEM] * 2 + [SPEC_ANY] * len(weights),
        scratch_shapes=[
            pltpu.VMEM(query_t.shape, BF16),
            pltpu.VMEM(key_t.shape, BF16),
            pltpu.VMEM((seqs, group, width), BF16),
            pltpu.VMEM((group, LAT), F32),
            pltpu.VMEM((group, 128), F32),
            pltpu.VMEM((group, 128), F32),
            pltpu.VMEM((rows_in, 128), F32),
            pltpu.SemaphoreType.DMA,
            pltpu.SemaphoreType.DMA((seqs, ctx // (2 * CHUNK))),
            pltpu.SemaphoreType.DMA((len(weights),)),
        ],
        compiler_params=pltpu.CompilerParams(vmem_limit_bytes=26 * MIB),
        cost_estimate=pl.CostEstimate(
            flops=2 * seqs * group * ctx * (width + LAT),
            bytes_accessed=2 * seqs * ctx * width,
            transcendentals=seqs * group * ctx,
        ),
        name="attention",
    )(*[in_hbm(arg) for arg in (lengths, row_seq, row_pos, drafts, query_t, key_t, *weights)])


def merge_shares(logs):
    peak = functools.reduce(jnp.maximum, logs)
    shares = [jnp.exp2(log - peak) for log in logs]
    total = functools.reduce(jnp.add, shares)
    shares = [share / total for share in shares]
    rows = sum(share.shape[0] for share in shares)
    stacked = jnp.concatenate(shares + [jnp.zeros((128 - rows, 128), F32)], axis=0)
    return stacked.T, peak + jnp.log2(total)


def merge_pair_kernel(rows_in, heads, mine_ref, sibling_ref, *rest):
    outs, mix = rest[:-1], rest[-1]
    blocks = len(outs)
    body = blocks * rows_in * heads
    me = lax.axis_index("kv")
    chip, core = lax.div(me, 2), lax.rem(me, 2)
    parts = (mine_ref, sibling_ref)
    mix[...], log_sum = merge_shares([unpack_logs(part[body:, :], rows_in) for part in parts])
    spread = pack_logs(log_sum)
    for k in range(blocks):
        block = jnp.bitwise_xor(chip, k)
        share = mix[pl.ds(pl.multiple_of((2 * block + core) * heads, heads), heads), :]
        for r in range(rows_in):
            source = pl.ds(pl.multiple_of((block * rows_in + r) * heads, heads), heads)
            whole = jnp.zeros((heads, LAT), F32)
            for p in range(2):
                at = p * rows_in + r
                whole = whole + parts[p][source, :].astype(F32) * share[:, at : at + 1]
            outs[k][r * heads : (r + 1) * heads, :] = whole.astype(BF16)
        outs[k][rows_in * heads :, :] = spread


def merge_pair(rows_in, heads, mine, sibling):
    blocks = (mine.shape[0] - 16) // (rows_in * heads)
    message = jax.ShapeDtypeStruct((rows_in * heads + 16, LAT), BF16)
    return pl.pallas_call(
        functools.partial(merge_pair_kernel, rows_in, heads),
        out_shape=[message] * blocks,
        in_specs=[SPEC_VMEM] * 2,
        out_specs=[SPEC_VMEM] * blocks,
        scratch_shapes=[pltpu.VMEM((128, 128), F32)],
        compiler_params=pltpu.CompilerParams(vmem_limit_bytes=8 * MIB),
        name="merge_pair",
    )(mine, sibling)


def merge_values_kernel(rows_in, w_ref, *rest):
    parts = rest[:-3]
    out_ref, mix, latent = rest[-3:]
    heads = w_ref.shape[0]
    body = rows_in * heads
    me = lax.axis_index("kv")
    mix[...], _ = merge_shares([unpack_logs(part[body:, :], rows_in) for part in parts])
    share = mix[pl.ds(pl.multiple_of(me * heads, heads), heads), :]
    for r in range(rows_in):
        block = slice(r * heads, (r + 1) * heads)
        whole = jnp.zeros((heads, LAT), F32)
        for k, part in enumerate(parts):
            at = k * rows_in + r
            whole = whole + part[block, :].astype(F32) * share[:, at : at + 1]
        for c in range(LAT // 128):
            latent[c, block, :] = whole[:, c * 128 : (c + 1) * 128]
    for h in range(heads):
        pieces = [latent[c, pl.ds(h, rows_in, stride=heads), :] for c in range(LAT // 128)]
        rows = jnp.concatenate(pieces, axis=1).astype(BF16)
        out_ref[:, h * HD : (h + 1) * HD] = dot_f32(rows, w_ref[h]).astype(BF16)


def merge_values(rows_in, w_uv, parts):
    heads = w_uv.shape[0]
    return pl.pallas_call(
        functools.partial(merge_values_kernel, rows_in),
        out_shape=jax.ShapeDtypeStruct((rows_in, heads * HD), BF16),
        in_specs=[SPEC_VMEM] * (1 + len(parts)),
        out_specs=SPEC_VMEM,
        scratch_shapes=[pltpu.VMEM((128, 128), F32), pltpu.VMEM((LAT // 128, rows_in * heads, 128), F32)],
        compiler_params=pltpu.CompilerParams(vmem_limit_bytes=8 * MIB),
        name="merge_values",
    )(held(w_uv), *parts)


def core_span(side, half):
    core = lax.rem(lax.axis_index("kv"), 2)
    return pl.ds(pl.multiple_of((core if side == 0 else 1 - core) * half, half), half)


def project_theirs_kernel(flips, w_ref, *rest):
    parts = rest[:-3]
    rows_ref, theirs_ref, whole = rest[-3:]
    rows = parts[0].shape[0]
    at = lax.axis_index("dp")
    for k, part in zip(flips, parts):
        place = pl.ds(pl.multiple_of(jnp.bitwise_xor(at, k) * rows, rows), rows)
        whole[place, :] = part[...].astype(F32)
    stacked = whole[...].astype(BF16)
    rows_ref[...] = stacked
    theirs_ref[...] = dot_f32(stacked, w_ref[:, core_span(1, theirs_ref.shape[1])]).astype(BF16)


def project_mine_kernel(w_ref, rows_ref, mine_ref):
    mine_ref[...] = dot_f32(rows_ref[...], w_ref[:, core_span(0, mine_ref.shape[1])])


def project(weight, parts, flips, name):
    rows, depth = parts[0].shape
    rows = rows * len(parts)
    half = weight.shape[1] // 2
    params = pltpu.CompilerParams(vmem_limit_bytes=8 * MIB)
    cost = pl.CostEstimate(
        flops=2 * rows * depth * half, bytes_accessed=2 * depth * half, transcendentals=0
    )
    stacked, theirs = pl.pallas_call(
        functools.partial(project_theirs_kernel, flips),
        out_shape=[jax.ShapeDtypeStruct((rows, depth), BF16), jax.ShapeDtypeStruct((rows, half), BF16)],
        in_specs=[SPEC_VMEM] * (1 + len(parts)),
        out_specs=[SPEC_VMEM] * 2,
        scratch_shapes=[pltpu.VMEM((rows, depth), F32)],
        compiler_params=params,
        cost_estimate=cost,
        name=name + "_theirs",
    )(held(weight), *parts)
    mine = pl.pallas_call(
        project_mine_kernel,
        out_shape=jax.ShapeDtypeStruct((rows, half), F32),
        in_specs=[SPEC_VMEM] * 2,
        out_specs=SPEC_VMEM,
        compiler_params=params,
        cost_estimate=cost,
        name=name + "_mine",
    )(held(weight), stacked)
    return mine, theirs


def add_pair_kernel(mine_ref, sibling_ref, out_ref):
    out_ref[...] = (mine_ref[...] + sibling_ref[...].astype(F32)).astype(BF16)


def add_pair(mine, sibling):
    return pl.pallas_call(
        add_pair_kernel,
        out_shape=jax.ShapeDtypeStruct(mine.shape, BF16),
        in_specs=[SPEC_VMEM] * 2,
        out_specs=SPEC_VMEM,
        compiler_params=pltpu.CompilerParams(vmem_limit_bytes=4 * MIB),
        name="add_pair",
    )(mine, sibling)


def add_tree(parts):
    parts = [part[...].astype(F32) for part in parts]
    while len(parts) > 1:
        parts = [parts[i] + parts[i + 1] for i in range(0, len(parts), 2)]
    return parts[0]


def add_chips_kernel(base_ref, *rest):
    parts, out_ref = rest[:-1], rest[-1]
    half = out_ref.shape[1]
    base = base_ref[...]
    if base.shape[1] > half:
        core = lax.rem(lax.axis_index("kv"), 2)
        base = jnp.where(core == 0, base[:, :half].astype(F32), base[:, half:].astype(F32))
    out_ref[...] = (base.astype(F32) + add_tree(parts)).astype(BF16)


def add_chips(base, parts, name):
    return pl.pallas_call(
        add_chips_kernel,
        out_shape=jax.ShapeDtypeStruct(parts[0].shape, BF16),
        in_specs=[SPEC_VMEM] * (1 + len(parts)),
        out_specs=SPEC_VMEM,
        compiler_params=pltpu.CompilerParams(vmem_limit_bytes=4 * MIB),
        name=name,
    )(base, *parts)


def expand_half(side, gate_ref, up_ref, gain_ref, resid):
    half = resid.shape[1]
    span = core_span(side, half)
    scaled = (resid * gain_ref[:, span]).astype(BF16)
    square = jnp.sum(resid * resid, axis=1, keepdims=True)
    return dot_f32(scaled, gate_ref[span, :]), dot_f32(scaled, up_ref[span, :]), square


def expand_mine_kernel(gate_ref, up_ref, gain_ref, mine_ref, sums_ref, square_ref):
    width = gate_ref.shape[1]
    gate, up, square = expand_half(0, gate_ref, up_ref, gain_ref, mine_ref[...].astype(F32))
    sums_ref[:, :width] = gate
    sums_ref[:, width:] = up
    square_ref[...] = jnp.broadcast_to(square, square_ref.shape)


def expand_rest_kernel(gate_ref, up_ref, gain_ref, sibling_ref, sums_ref, square_ref, *rest):
    outs, total = rest[:-1], rest[-1]
    rows = outs[0].shape[0]
    width = gate_ref.shape[1]
    at = lax.axis_index("dp")
    gate, up, square = expand_half(1, gate_ref, up_ref, gain_ref, sibling_ref[...].astype(F32))
    total[:, :width] = sums_ref[:, :width] + gate
    total[:, width : 2 * width] = sums_ref[:, width:] + up
    lane = lax.broadcasted_iota(jnp.int32, square_ref.shape, 1)
    terms = three_terms(square_ref[...] + square)
    tail = jnp.zeros(lane.shape, F32)
    for t in range(3):
        tail = jnp.where(lane == t, terms[t], tail)
    total[:, 2 * width :] = tail
    for k in range(len(outs)):
        place = pl.ds(pl.multiple_of(jnp.bitwise_xor(at, k) * rows, rows), rows)
        outs[k][...] = total[place, :].astype(BF16)


def expand(dp_count, w_gate, w_up, gain, mine, sibling):
    cols, width = w_gate.shape
    rows = mine.shape[0]
    params = pltpu.CompilerParams(vmem_limit_bytes=8 * MIB)
    cost = pl.CostEstimate(
        flops=2 * rows * cols * width, bytes_accessed=2 * cols * width, transcendentals=0
    )
    weights = (held(w_gate), held(w_up), gain.reshape(1, cols))
    sums, square = pl.pallas_call(
        expand_mine_kernel,
        out_shape=[
            jax.ShapeDtypeStruct((rows, 2 * width), F32),
            jax.ShapeDtypeStruct((rows, 128), F32),
        ],
        in_specs=[SPEC_VMEM] * 4,
        out_specs=[SPEC_VMEM] * 2,
        compiler_params=params,
        cost_estimate=cost,
        name="gate_up_mine",
    )(*weights, mine)
    message = jax.ShapeDtypeStruct((rows // dp_count, 2 * width + 128), BF16)
    return pl.pallas_call(
        expand_rest_kernel,
        out_shape=[message] * dp_count,
        in_specs=[SPEC_VMEM] * 6,
        out_specs=[SPEC_VMEM] * dp_count,
        scratch_shapes=[pltpu.VMEM((rows, 2 * width + 128), F32)],
        compiler_params=params,
        cost_estimate=cost,
        name="gate_up_rest",
    )(*weights, sibling, sums, square)


def activate_kernel(*rest):
    parts, out_ref = rest[:-1], rest[-1]
    width = out_ref.shape[1]
    total = functools.reduce(jnp.add, [part[...].astype(F32) for part in parts])
    square = jnp.sum(total[:, 2 * width :], axis=1, keepdims=True)
    inv_rms = lax.rsqrt(square / D + 1e-06)
    gate = total[:, :width] * inv_rms
    up = total[:, width : 2 * width] * inv_rms
    out_ref[...] = (gate / (1.0 + jnp.exp(-gate)) * up).astype(BF16)


def activate(parts):
    rows, wide = parts[0].shape
    return pl.pallas_call(
        activate_kernel,
        out_shape=jax.ShapeDtypeStruct((rows, (wide - 128) // 2), BF16),
        in_specs=[SPEC_VMEM] * len(parts),
        out_specs=SPEC_VMEM,
        compiler_params=pltpu.CompilerParams(vmem_limit_bytes=4 * MIB),
        name="activate",
    )(*parts)


def assemble_kernel(mine_ref, sibling_ref, out_ref):
    half = mine_ref.shape[1]
    left = lax.rem(lax.axis_index("kv"), 2) == 0
    mine, sibling = mine_ref[...].astype(F32), sibling_ref[...].astype(F32)
    out_ref[:, :half] = jnp.where(left, mine, sibling).astype(BF16)
    out_ref[:, half:] = jnp.where(left, sibling, mine).astype(BF16)


def assemble(mine, sibling):
    rows, half = mine.shape
    return pl.pallas_call(
        assemble_kernel,
        out_shape=jax.ShapeDtypeStruct((rows, 2 * half), BF16),
        in_specs=[SPEC_VMEM] * 2,
        out_specs=SPEC_VMEM,
        compiler_params=pltpu.CompilerParams(vmem_limit_bytes=4 * MIB),
        name="assemble",
    )(mine, sibling)


def partner(array, axis, flip):
    pairs = [(i, i ^ flip) for i in range(lax.axis_size(axis))]
    return lax.ppermute(array, axis, pairs)


def swap(parts, axis, unit, flips):
    return [partner(parts[k], axis, k * unit) if k else parts[0] for k in flips]


def line_flips(count):
    return [*range(2, count), 1, 0]


def grid_flips(count):
    return list(range(count - 1, -1, -1))


def sum_over_kv(weight, parts, flips, base, name):
    chips = lax.axis_size("kv") // 2
    mine, theirs = project(weight, parts, flips, name)
    pair = add_pair(mine, partner(theirs, "kv", 1))
    half = add_chips(base, swap([pair] * chips, "kv", 2, range(chips)), name + "_sum")
    return half, partner(half, "kv", 1)


def on_device_tiled(
    queries, drafts, cache, lengths, row_seq, row_pos, w_uv, w_out, hidden, gain, w_gate, w_up, w_down
):
    kv_count = lax.axis_size("kv")
    dp_count = lax.axis_size("dp")
    rows_in, head_count = queries.shape[:2]
    flips = line_flips(dp_count)
    query_t = jnp.swapaxes(queries, 1, 2)
    key_t = jnp.swapaxes(cache, 1, 2)
    mine, theirs, w_uv, w_out, w_gate, w_up = attention(
        kv_count, lengths, row_seq, row_pos, drafts, query_t, key_t, [w_uv, w_out, w_gate, w_up]
    )
    blocks = merge_pair(rows_in, head_count // kv_count, mine, partner(theirs, "kv", 1))
    values = merge_values(rows_in, w_uv, swap(blocks, "kv", 2, grid_flips(len(blocks))))
    resid, resid_sibling = sum_over_kv(w_out, swap([values] * dp_count, "dp", 1, flips), flips, hidden, "project_out")
    sums = expand(dp_count, w_gate, w_up, gain, resid, resid_sibling)
    act = activate(swap(sums, "dp", 1, flips))
    mixed, mixed_sibling = sum_over_kv(w_down, swap([act] * dp_count, "dp", 1, flips), flips, resid, "project_down")
    return assemble(mixed, mixed_sibling)


def tiles_fit(kv_count, dp_count, head_count, rows_in, cols, ctx):
    powers = kv_count & (kv_count - 1) == 0 and dp_count & (dp_count - 1) == 0
    heads = head_count % (16 * kv_count) == 0 and head_count == 128 and kv_count * rows_in <= 128
    return powers and heads and rows_in == 8 and cols % 256 == 0 and ctx % (2 * CHUNK) == 0


def solution(mesh):
    placed = (
        P("dp", None, None),
        P("dp", None),
        P("dp", "kv", None),
        P("dp"),
        P("dp"),
        P("dp"),
        P("kv", None, None),
        P("kv", "dp"),
        P(None, "dp"),
        P("dp"),
        P("dp", "kv"),
        P("dp", "kv"),
        P("kv", "dp"),
    )

    def placed_call(body):
        return jax.shard_map(
            body, mesh=mesh, in_specs=placed, out_specs=P(None, "dp"), check_vma=False
        )

    def run(*args):
        kv_count, dp_count = mesh.shape["kv"], mesh.shape["dp"]
        queries, cache, hidden = args[0], args[2], args[8]
        fits = tiles_fit(
            kv_count,
            dp_count,
            queries.shape[1],
            queries.shape[0] // dp_count,
            hidden.shape[1] // dp_count,
            cache.shape[1] // kv_count,
        )
        return placed_call(on_device_tiled if fits else on_device)(*args)

    return run
```

```python
import functools

import jax
import jax.numpy as jnp
from jax import lax
from jax.experimental import pallas as pl
from jax.experimental.pallas import tpu as pltpu
from jax.sharding import PartitionSpec as P

D = 7168
LAT = 512
ROPE = 64
HD = 128
SEQ_DP = 2
STEPS = 4


def scan_cache(query_rows, key_rows, live_len, block_len, block_count):
    qk_scale = (HD + ROPE) ** (-0.5)
    row_count = query_rows.shape[0]

    def visit(block_idx, carry):
        run_max, run_sum, weighted = carry
        key_block = lax.dynamic_slice_in_dim(key_rows, block_idx * block_len, block_len, 0)
        scores = (
            jnp.einsum("rc,kc->rk", query_rows, key_block, preferred_element_type=jnp.float32)
            * qk_scale
        )
        valid = block_idx * block_len + jnp.arange(block_len) < live_len
        scores = jnp.where(valid[None, :], scores, -1e30)
        new_max = jnp.maximum(run_max, jnp.max(scores, axis=1))
        weights = jnp.where(valid[None, :], jnp.exp(scores - new_max[:, None]), 0.0)
        factor = jnp.exp(run_max - new_max)
        run_sum = run_sum * factor + jnp.sum(weights, axis=1)
        weighted = weighted * factor[:, None] + jnp.dot(
            weights.astype(jnp.bfloat16), key_block[:, :LAT], preferred_element_type=jnp.float32
        )
        return (new_max, run_sum, weighted)

    start_carry = (
        jnp.full((row_count,), -1e30, jnp.float32),
        jnp.zeros((row_count,), jnp.float32),
        jnp.zeros((row_count, LAT), jnp.float32),
    )
    return lax.fori_loop(0, block_count, visit, start_carry)


def on_device(
    queries,
    drafts,
    cache,
    lengths,
    row_seq,
    row_pos,
    w_uv,
    w_out,
    hidden,
    gain,
    w_gate,
    w_up,
    w_down,
):
    kv_count = lax.axis_size("kv")
    kv_index = lax.axis_index("kv")
    tok_group, head_count = (queries.shape[0], queries.shape[1])
    head_local = head_count // kv_count
    ctx_dev = cache.shape[1]
    shard_start = kv_index * ctx_dev
    block_len = min(512, ctx_dev)
    block_total = ctx_dev // block_len
    qk_scale = (HD + ROPE) ** (-0.5)
    order_idx = jnp.arange(tok_group)
    same_seq = row_seq[:, None] == row_seq[None, :]
    rank_in_seq = jnp.sum(same_seq & (order_idx[:, None] > order_idx[None, :]), axis=1)
    picker = (row_seq[None, None, :] == jnp.arange(SEQ_DP)[:, None, None]) & (
        rank_in_seq[None, None, :] == jnp.arange(STEPS)[None, :, None]
    )
    picker_b = picker.astype(jnp.bfloat16)
    sorted_q = jnp.einsum(
        "sri,ihc->srhc", picker_b, queries, preferred_element_type=jnp.float32
    ).astype(jnp.bfloat16)
    sorted_drafts = (
        jnp.einsum("sri,ic->src", picker_b, drafts, preferred_element_type=jnp.float32)
        .astype(jnp.bfloat16)
        .reshape(tok_group, -1)
    )
    sorted_pos = jnp.sum(jnp.where(picker, row_pos[None, None, :], 0), axis=2).reshape(-1)
    sorted_seq = jnp.repeat(jnp.arange(SEQ_DP), STEPS)
    max_parts, sum_parts, acc_parts = ([], [], [])
    for seq_idx in range(SEQ_DP):
        live_len = lengths[seq_idx] - shard_start
        query_rows = sorted_q[seq_idx].reshape(STEPS * head_count, -1)
        run_max, run_sum, weighted = scan_cache(
            query_rows, cache[seq_idx], live_len, block_len, block_total
        )
        max_parts.append(run_max.reshape(STEPS, head_count))
        sum_parts.append(run_sum.reshape(STEPS, head_count))
        acc_parts.append(weighted.reshape(STEPS, head_count, LAT))
    local_max = jnp.concatenate(max_parts, axis=0)
    local_sum = jnp.concatenate(sum_parts, axis=0)
    local_acc = jnp.concatenate(acc_parts, axis=0)
    recv_acc, recv_max, recv_sum = (
        lax.all_to_all(local_acc[None], "kv", split_axis=2, concat_axis=0, tiled=True),
        lax.all_to_all(local_max[None], "kv", split_axis=2, concat_axis=0, tiled=True),
        lax.all_to_all(local_sum[None], "kv", split_axis=2, concat_axis=0, tiled=True),
    )
    head_max = jnp.max(recv_max, axis=0)
    rescale = jnp.exp(recv_max - head_max[None])
    head_acc = jnp.sum(recv_acc * rescale[..., None], axis=0)
    head_sum = jnp.sum(recv_sum * rescale, axis=0)
    head_q = lax.dynamic_slice_in_dim(
        sorted_q.reshape(tok_group, head_count, -1), kv_index * head_local, head_local, 1
    )
    draft_scores = (
        jnp.einsum("thc,jc->thj", head_q, sorted_drafts, preferred_element_type=jnp.float32)
        * qk_scale
    )
    draft_valid = (sorted_seq[:, None] == sorted_seq[None, :]) & (
        sorted_pos[None, :] <= sorted_pos[:, None]
    )
    draft_scores = jnp.where(draft_valid[:, None, :], draft_scores, -1e30)
    final_max = jnp.maximum(head_max, jnp.max(draft_scores, axis=2))
    adjust = jnp.exp(head_max - final_max)
    draft_weight = jnp.where(
        draft_valid[:, None, :], jnp.exp(draft_scores - final_max[:, :, None]), 0.0
    )
    denom = head_sum * adjust + jnp.sum(draft_weight, axis=2)
    numer = head_acc * adjust[:, :, None] + jnp.einsum(
        "thj,jl->thl",
        draft_weight.astype(jnp.bfloat16),
        sorted_drafts[:, :LAT],
        preferred_element_type=jnp.float32,
    )
    latent_sorted = (
        (numer / denom[:, :, None]).astype(jnp.bfloat16).reshape(SEQ_DP, STEPS, head_local, LAT)
    )
    latent_rows = jnp.einsum(
        "sri,srhl->ihl", picker_b, latent_sorted, preferred_element_type=jnp.float32
    ).astype(jnp.bfloat16)
    all_latents = lax.all_gather(latent_rows, "dp", axis=0, tiled=True)
    all_values = jnp.einsum(
        "thl,hlv->thv", all_latents, w_uv, preferred_element_type=jnp.float32
    ).astype(jnp.bfloat16)
    row_total = all_values.shape[0]
    attn_part = jnp.dot(
        all_values.reshape(row_total, head_local * HD), w_out, preferred_element_type=jnp.float32
    )
    attended = lax.psum(attn_part, "kv")
    resid = (hidden.astype(jnp.float32) + attended).astype(jnp.bfloat16)
    resid_f = resid.astype(jnp.float32)
    square_part = jnp.sum(resid_f * resid_f, axis=1)
    scaled = (resid_f * gain[None, :]).astype(jnp.bfloat16)
    gate_part = jnp.dot(scaled, w_gate, preferred_element_type=jnp.float32)
    up_part = jnp.dot(scaled, w_up, preferred_element_type=jnp.float32)
    gate_sum, up_sum, square_sum = lax.psum((gate_part, up_part, square_part), "dp")
    inv_rms = lax.rsqrt(square_sum / D + 1e-06)[:, None]
    act = (jax.nn.silu(gate_sum * inv_rms) * (up_sum * inv_rms)).astype(jnp.bfloat16)
    down_part = jnp.dot(act, w_down, preferred_element_type=jnp.float32)
    down_sum = lax.psum(down_part, "kv")
    return (resid_f + down_sum).astype(jnp.bfloat16)


CHUNK = 1024
MASKED = -1e30
F32 = jnp.float32
BF16 = jnp.bfloat16
SPEC_VMEM = pl.BlockSpec(memory_space=pltpu.VMEM)
SPEC_SMEM = pl.BlockSpec(memory_space=pltpu.SMEM)
SPEC_ANY = pl.BlockSpec(memory_space=pl.ANY)
MIB = 1024 * 1024


def dot_f32(lhs, rhs, contract=((1,), (0,))):
    return lax.dot_general(lhs, rhs, (contract, ((), ())), preferred_element_type=F32)


def held(array):
    return pltpu.with_memory_space_constraint(array, pltpu.VMEM)


def in_hbm(array):
    return pltpu.with_memory_space_constraint(array, pltpu.HBM)


def three_terms(exact):
    high = exact.astype(BF16).astype(F32)
    middle = (exact - high).astype(BF16).astype(F32)
    low = (exact - high - middle).astype(BF16).astype(F32)
    return high, middle, low


def pack_logs(logs):
    spread = jnp.concatenate(three_terms(logs) + (jnp.zeros_like(logs),), axis=1)
    return jnp.concatenate([spread, jnp.zeros_like(spread)], axis=0).astype(BF16)


def unpack_logs(spread, rows_in):
    spread = spread.astype(F32)[:rows_in, :]
    return spread[:, :128] + spread[:, 128:256] + spread[:, 256:384]


def attention_kernel(
    kv_count, weight_count, len_ref, seq_ref, pos_ref, draft_ref, query_hbm, key_hbm, *rest
):
    weights_hbm = rest[:weight_count]
    mine_ref, theirs_ref = rest[weight_count : weight_count + 2]
    weights_ref = rest[weight_count + 2 : 2 * weight_count + 2]
    (query_t, keys, query_s, acc, row_max, row_sum, logs, query_sem, key_sem, weight_sem) = rest[
        2 * weight_count + 2 :
    ]
    rows_in, width, head_count = query_hbm.shape
    seqs, _, ctx = key_hbm.shape
    steps = rows_in // seqs
    head_local = head_count // kv_count
    lat = acc.shape[1]
    pair = 2 * CHUNK
    pair_total = ctx // pair
    factor = (HD + ROPE) ** (-0.5) * 1.4426950408889634
    me = lax.axis_index("kv")
    core = lax.rem(me, 2)

    query_copy = pltpu.make_async_copy(query_hbm, query_t, query_sem)
    query_copy.start()

    def key_copy(s, j):
        cols = pl.ds(pl.multiple_of(j * pair, pair), pair)
        return pltpu.make_async_copy(key_hbm.at[s, :, cols], keys.at[s, :, cols], key_sem.at[s, j])

    later_copies = [key_copy(s, j) for s in range(seqs) for j in range(pair_total)]
    later_copies.pop(0).start()
    weight_copies = [
        pltpu.make_async_copy(weights_hbm[w], weights_ref[w], weight_sem.at[w]) for w in range(weight_count)
    ]

    row_of = []
    for s in range(seqs):
        found = jnp.int32(0)
        slots = [jnp.int32(0)] * steps
        for r in range(rows_in):
            mine = seq_ref[r] == s
            slots = [jnp.where(mine & (found == i), r, slots[i]) for i in range(steps)]
            found = found + mine.astype(jnp.int32)
        row_of.append(slots)

    query_copy.wait()
    for copy in later_copies:
        copy.start()
    for s in range(seqs):
        for i in range(steps):
            query_s[s, i * head_count : (i + 1) * head_count, :] = query_t[row_of[s][i]].T

    row_iota = lax.broadcasted_iota(jnp.int32, (rows_in, 128), 0)
    owner = me == kv_count - 1
    logs[...] = jnp.zeros_like(logs)

    for s in range(seqs):

        @pl.when(jnp.logical_not(owner))
        def start_empty():
            row_max[...] = jnp.full_like(row_max, MASKED)
            row_sum[...] = jnp.zeros_like(row_sum)
            acc[...] = jnp.zeros_like(acc)

        @pl.when(owner)
        def start_drafts():
            draft_pad = jnp.concatenate(
                [draft_ref[...].astype(F32), jnp.zeros((128 - rows_in, width), F32)], axis=0
            ).astype(BF16)
            lane = lax.broadcasted_iota(jnp.int32, (1, 128), 1)
            score = dot_f32(query_s[s], draft_pad, ((1,), (1,)))
            masks = []
            for i in range(steps):
                admitted = jnp.zeros((1, 128), jnp.int32)
                for r in range(rows_in):
                    fits = (seq_ref[r] == s) & (pos_ref[r] <= pos_ref[row_of[s][i]])
                    admitted = jnp.where(lane == r, fits.astype(jnp.int32), admitted)
                masks.append(jnp.broadcast_to(admitted, (head_count, 128)))
            mask = jnp.concatenate(masks, axis=0) > 0
            score = jnp.where(mask, score, MASKED)
            first_max = jnp.broadcast_to(jnp.max(score, axis=1, keepdims=True), score.shape)
            weight = jnp.where(mask, jnp.exp2((score - first_max) * factor), 0.0)
            row_max[...] = first_max
            row_sum[...] = weight
            acc[...] = dot_f32(weight.astype(BF16), draft_pad[:, :lat])

        live = jnp.clip(len_ref[s] - me * ctx, 0, ctx)
        live_pairs = lax.div(live + (pair - 1), pair)

        def add_block(base, masked):
            halves = [pl.ds(base, CHUNK), pl.ds(base + CHUNK, CHUNK)]
            scores = [dot_f32(query_s[s], keys[s, :, half]) for half in halves]
            for h in range(2):
                score = scores[h]
                if masked:
                    place = base + h * CHUNK + lax.broadcasted_iota(jnp.int32, (1, CHUNK), 1)
                    score = jnp.where(place < live, score, MASKED)
                old_max = row_max[...]
                new_max = jnp.maximum(old_max, jnp.max(score, axis=1, keepdims=True))
                scale = jnp.exp2((old_max - new_max) * factor)
                weight = jnp.exp2(score * factor - jnp.concatenate([new_max * factor] * (CHUNK // 128), axis=1))
                part = weight[:, :128]
                for c in range(1, CHUNK // 128):
                    part = part + weight[:, c * 128 : (c + 1) * 128]
                row_max[...] = new_max
                row_sum[...] = row_sum[...] * scale + part
                update = dot_f32(weight.astype(BF16), keys[s, :lat, halves[h]], ((1,), (1,)))
                acc[...] = acc[...] * jnp.concatenate([scale] * (lat // 128), axis=1) + update

        def visit(j, carry):
            key_copy(s, j).wait()
            if s == 0:
                for w in range(weight_count):
                    @pl.when(j == w % pair_total)
                    def start_weight():
                        weight_copies[w].start()
            base = pl.multiple_of(j * pair, pair)
            whole = base + pair <= live

            @pl.when(whole)
            def all_live():
                add_block(base, False)

            @pl.when(jnp.logical_not(whole))
            def some_live():
                add_block(base, True)

            return carry

        lax.fori_loop(0, live_pairs, visit, 0)

        def skip(j, carry):
            key_copy(s, j).wait()
            return carry

        lax.fori_loop(live_pairs, pair_total, skip, 0)
        if s == 0:
            for w in range(weight_count):
                @pl.when(live_pairs <= w % pair_total)
                def start_weight():
                    weight_copies[w].start()

        total = jnp.sum(row_sum[...], axis=1, keepdims=True)
        some = total > 0.0
        acc[...] = acc[...] * jnp.where(some, 1.0 / jnp.where(some, total, 1.0), 0.0)
        log_sum = jnp.where(
            some, row_max[...] * factor + jnp.log2(jnp.where(some, total, 1.0)), MASKED
        )
        for i in range(steps):
            flat = log_sum[i * head_count : (i + 1) * head_count, :].T[:1, :]
            logs[...] = jnp.where(row_iota == row_of[s][i], flat, logs[...])
            for b in range(kv_count // 2):
                base = (b * rows_in + row_of[s][i]) * head_local
                target = pl.ds(pl.multiple_of(base, head_local), head_local)
                for ref, side in ((mine_ref, core), (theirs_ref, 1 - core)):
                    start = i * head_count + (2 * b + side) * head_local
                    source = pl.ds(pl.multiple_of(start, head_local), head_local)
                    ref[target, :] = acc[source, :].astype(BF16)

    spread = pack_logs(logs[...])
    body = rows_in * head_count // 2
    mine_ref[body:, :] = spread
    theirs_ref[body:, :] = spread
    for copy in weight_copies:
        copy.wait()


def attention(kv_count, lengths, row_seq, row_pos, drafts, query_t, key_t, weights):
    rows_in, width, head_count = query_t.shape
    seqs, _, ctx = key_t.shape
    group = rows_in // seqs * head_count
    message = pltpu.VMEM((rows_in * head_count // 2 + 16, LAT), BF16)
    return pl.pallas_call(
        functools.partial(attention_kernel, kv_count, len(weights)),
        out_shape=[message] * 2 + [pltpu.VMEM(weight.shape, weight.dtype) for weight in weights],
        in_specs=[SPEC_SMEM] * 3 + [SPEC_VMEM] + [SPEC_ANY] * (2 + len(weights)),
        out_specs=[SPEC_VMEM] * 2 + [SPEC_ANY] * len(weights),
        scratch_shapes=[
            pltpu.VMEM(query_t.shape, BF16),
            pltpu.VMEM(key_t.shape, BF16),
            pltpu.VMEM((seqs, group, width), BF16),
            pltpu.VMEM((group, LAT), F32),
            pltpu.VMEM((group, 128), F32),
            pltpu.VMEM((group, 128), F32),
            pltpu.VMEM((rows_in, 128), F32),
            pltpu.SemaphoreType.DMA,
            pltpu.SemaphoreType.DMA((seqs, ctx // (2 * CHUNK))),
            pltpu.SemaphoreType.DMA((len(weights),)),
        ],
        compiler_params=pltpu.CompilerParams(vmem_limit_bytes=26 * MIB),
        cost_estimate=pl.CostEstimate(
            flops=2 * seqs * group * ctx * (width + LAT),
            bytes_accessed=2 * seqs * ctx * width,
            transcendentals=seqs * group * ctx,
        ),
        name="attention",
    )(*[in_hbm(arg) for arg in (lengths, row_seq, row_pos, drafts, query_t, key_t, *weights)])


def merge_shares(logs):
    peak = functools.reduce(jnp.maximum, logs)
    shares = [jnp.exp2(log - peak) for log in logs]
    total = functools.reduce(jnp.add, shares)
    shares = [share / total for share in shares]
    rows = sum(share.shape[0] for share in shares)
    stacked = jnp.concatenate(shares + [jnp.zeros((128 - rows, 128), F32)], axis=0)
    return stacked.T, peak + jnp.log2(total)


def merge_pair_kernel(rows_in, heads, mine_ref, sibling_ref, *rest):
    outs, mix = rest[:-1], rest[-1]
    blocks = len(outs)
    body = blocks * rows_in * heads
    me = lax.axis_index("kv")
    chip, core = lax.div(me, 2), lax.rem(me, 2)
    parts = (mine_ref, sibling_ref)
    mix[...], log_sum = merge_shares([unpack_logs(part[body:, :], rows_in) for part in parts])
    spread = pack_logs(log_sum)
    for k in range(blocks):
        block = jnp.bitwise_xor(chip, k)
        share = mix[pl.ds(pl.multiple_of((2 * block + core) * heads, heads), heads), :]
        for r in range(rows_in):
            source = pl.ds(pl.multiple_of((block * rows_in + r) * heads, heads), heads)
            whole = jnp.zeros((heads, LAT), F32)
            for p in range(2):
                at = p * rows_in + r
                whole = whole + parts[p][source, :].astype(F32) * share[:, at : at + 1]
            outs[k][r * heads : (r + 1) * heads, :] = whole.astype(BF16)
        outs[k][rows_in * heads :, :] = spread


def merge_pair(rows_in, heads, mine, sibling):
    blocks = (mine.shape[0] - 16) // (rows_in * heads)
    message = jax.ShapeDtypeStruct((rows_in * heads + 16, LAT), BF16)
    return pl.pallas_call(
        functools.partial(merge_pair_kernel, rows_in, heads),
        out_shape=[message] * blocks,
        in_specs=[SPEC_VMEM] * 2,
        out_specs=[SPEC_VMEM] * blocks,
        scratch_shapes=[pltpu.VMEM((128, 128), F32)],
        compiler_params=pltpu.CompilerParams(vmem_limit_bytes=8 * MIB),
        name="merge_pair",
    )(mine, sibling)


def merge_values_kernel(rows_in, w_ref, *rest):
    parts = rest[:-3]
    out_ref, mix, latent = rest[-3:]
    heads = w_ref.shape[0]
    body = rows_in * heads
    me = lax.axis_index("kv")
    mix[...], _ = merge_shares([unpack_logs(part[body:, :], rows_in) for part in parts])
    share = mix[pl.ds(pl.multiple_of(me * heads, heads), heads), :]
    for r in range(rows_in):
        block = slice(r * heads, (r + 1) * heads)
        whole = jnp.zeros((heads, LAT), F32)
        for k, part in enumerate(parts):
            at = k * rows_in + r
            whole = whole + part[block, :].astype(F32) * share[:, at : at + 1]
        for c in range(LAT // 128):
            latent[c, block, :] = whole[:, c * 128 : (c + 1) * 128]
    for h in range(heads):
        pieces = [latent[c, pl.ds(h, rows_in, stride=heads), :] for c in range(LAT // 128)]
        rows = jnp.concatenate(pieces, axis=1).astype(BF16)
        out_ref[:, h * HD : (h + 1) * HD] = dot_f32(rows, w_ref[h]).astype(BF16)


def merge_values(rows_in, w_uv, parts):
    heads = w_uv.shape[0]
    return pl.pallas_call(
        functools.partial(merge_values_kernel, rows_in),
        out_shape=jax.ShapeDtypeStruct((rows_in, heads * HD), BF16),
        in_specs=[SPEC_VMEM] * (1 + len(parts)),
        out_specs=SPEC_VMEM,
        scratch_shapes=[pltpu.VMEM((128, 128), F32), pltpu.VMEM((LAT // 128, rows_in * heads, 128), F32)],
        compiler_params=pltpu.CompilerParams(vmem_limit_bytes=8 * MIB),
        name="merge_values",
    )(held(w_uv), *parts)


def core_span(side, half):
    core = lax.rem(lax.axis_index("kv"), 2)
    return pl.ds(pl.multiple_of((core if side == 0 else 1 - core) * half, half), half)


def project_theirs_kernel(flips, w_ref, *rest):
    parts = rest[:-3]
    rows_ref, theirs_ref, whole = rest[-3:]
    rows = parts[0].shape[0]
    at = lax.axis_index("dp")
    for k, part in zip(flips, parts):
        place = pl.ds(pl.multiple_of(jnp.bitwise_xor(at, k) * rows, rows), rows)
        whole[place, :] = part[...].astype(F32)
    stacked = whole[...].astype(BF16)
    rows_ref[...] = stacked
    theirs_ref[...] = dot_f32(stacked, w_ref[:, core_span(1, theirs_ref.shape[1])]).astype(BF16)


def project_mine_kernel(w_ref, rows_ref, mine_ref):
    mine_ref[...] = dot_f32(rows_ref[...], w_ref[:, core_span(0, mine_ref.shape[1])])


def project(weight, parts, flips, name):
    rows, depth = parts[0].shape
    rows = rows * len(parts)
    half = weight.shape[1] // 2
    params = pltpu.CompilerParams(vmem_limit_bytes=8 * MIB)
    cost = pl.CostEstimate(
        flops=2 * rows * depth * half, bytes_accessed=2 * depth * half, transcendentals=0
    )
    stacked, theirs = pl.pallas_call(
        functools.partial(project_theirs_kernel, flips),
        out_shape=[jax.ShapeDtypeStruct((rows, depth), BF16), jax.ShapeDtypeStruct((rows, half), BF16)],
        in_specs=[SPEC_VMEM] * (1 + len(parts)),
        out_specs=[SPEC_VMEM] * 2,
        scratch_shapes=[pltpu.VMEM((rows, depth), F32)],
        compiler_params=params,
        cost_estimate=cost,
        name=name + "_theirs",
    )(held(weight), *parts)
    mine = pl.pallas_call(
        project_mine_kernel,
        out_shape=jax.ShapeDtypeStruct((rows, half), F32),
        in_specs=[SPEC_VMEM] * 2,
        out_specs=SPEC_VMEM,
        compiler_params=params,
        cost_estimate=cost,
        name=name + "_mine",
    )(held(weight), stacked)
    return mine, theirs


def add_pair_kernel(mine_ref, sibling_ref, out_ref):
    out_ref[...] = (mine_ref[...] + sibling_ref[...].astype(F32)).astype(BF16)


def add_pair(mine, sibling):
    return pl.pallas_call(
        add_pair_kernel,
        out_shape=jax.ShapeDtypeStruct(mine.shape, BF16),
        in_specs=[SPEC_VMEM] * 2,
        out_specs=SPEC_VMEM,
        compiler_params=pltpu.CompilerParams(vmem_limit_bytes=4 * MIB),
        name="add_pair",
    )(mine, sibling)


def add_tree(parts):
    parts = [part[...].astype(F32) for part in parts]
    while len(parts) > 1:
        parts = [parts[i] + parts[i + 1] for i in range(0, len(parts), 2)]
    return parts[0]


def add_chips_kernel(base_ref, *rest):
    parts, out_ref = rest[:-1], rest[-1]
    half = out_ref.shape[1]
    base = base_ref[...]
    if base.shape[1] > half:
        core = lax.rem(lax.axis_index("kv"), 2)
        base = jnp.where(core == 0, base[:, :half].astype(F32), base[:, half:].astype(F32))
    out_ref[...] = (base.astype(F32) + add_tree(parts)).astype(BF16)


def add_chips(base, parts, name):
    return pl.pallas_call(
        add_chips_kernel,
        out_shape=jax.ShapeDtypeStruct(parts[0].shape, BF16),
        in_specs=[SPEC_VMEM] * (1 + len(parts)),
        out_specs=SPEC_VMEM,
        compiler_params=pltpu.CompilerParams(vmem_limit_bytes=4 * MIB),
        name=name,
    )(base, *parts)


def expand_half(side, gate_ref, up_ref, gain_ref, resid):
    half = resid.shape[1]
    span = core_span(side, half)
    scaled = (resid * gain_ref[:, span]).astype(BF16)
    square = jnp.sum(resid * resid, axis=1, keepdims=True)
    return dot_f32(scaled, gate_ref[span, :]), dot_f32(scaled, up_ref[span, :]), square


def expand_mine_kernel(gate_ref, up_ref, gain_ref, mine_ref, sums_ref, square_ref):
    width = gate_ref.shape[1]
    gate, up, square = expand_half(0, gate_ref, up_ref, gain_ref, mine_ref[...].astype(F32))
    sums_ref[:, :width] = gate
    sums_ref[:, width:] = up
    square_ref[...] = jnp.broadcast_to(square, square_ref.shape)


def expand_rest_kernel(gate_ref, up_ref, gain_ref, sibling_ref, sums_ref, square_ref, *rest):
    outs, total = rest[:-1], rest[-1]
    rows = outs[0].shape[0]
    width = gate_ref.shape[1]
    at = lax.axis_index("dp")
    gate, up, square = expand_half(1, gate_ref, up_ref, gain_ref, sibling_ref[...].astype(F32))
    total[:, :width] = sums_ref[:, :width] + gate
    total[:, width : 2 * width] = sums_ref[:, width:] + up
    lane = lax.broadcasted_iota(jnp.int32, square_ref.shape, 1)
    terms = three_terms(square_ref[...] + square)
    tail = jnp.zeros(lane.shape, F32)
    for t in range(3):
        tail = jnp.where(lane == t, terms[t], tail)
    total[:, 2 * width :] = tail
    for k in range(len(outs)):
        place = pl.ds(pl.multiple_of(jnp.bitwise_xor(at, k) * rows, rows), rows)
        outs[k][...] = total[place, :].astype(BF16)


def expand(dp_count, w_gate, w_up, gain, mine, sibling):
    cols, width = w_gate.shape
    rows = mine.shape[0]
    params = pltpu.CompilerParams(vmem_limit_bytes=8 * MIB)
    cost = pl.CostEstimate(
        flops=2 * rows * cols * width, bytes_accessed=2 * cols * width, transcendentals=0
    )
    weights = (held(w_gate), held(w_up), gain.reshape(1, cols))
    sums, square = pl.pallas_call(
        expand_mine_kernel,
        out_shape=[
            jax.ShapeDtypeStruct((rows, 2 * width), F32),
            jax.ShapeDtypeStruct((rows, 128), F32),
        ],
        in_specs=[SPEC_VMEM] * 4,
        out_specs=[SPEC_VMEM] * 2,
        compiler_params=params,
        cost_estimate=cost,
        name="gate_up_mine",
    )(*weights, mine)
    message = jax.ShapeDtypeStruct((rows // dp_count, 2 * width + 128), BF16)
    return pl.pallas_call(
        expand_rest_kernel,
        out_shape=[message] * dp_count,
        in_specs=[SPEC_VMEM] * 6,
        out_specs=[SPEC_VMEM] * dp_count,
        scratch_shapes=[pltpu.VMEM((rows, 2 * width + 128), F32)],
        compiler_params=params,
        cost_estimate=cost,
        name="gate_up_rest",
    )(*weights, sibling, sums, square)


def activate_kernel(*rest):
    parts, out_ref = rest[:-1], rest[-1]
    width = out_ref.shape[1]
    total = functools.reduce(jnp.add, [part[...].astype(F32) for part in parts])
    square = jnp.sum(total[:, 2 * width :], axis=1, keepdims=True)
    inv_rms = lax.rsqrt(square / D + 1e-06)
    gate = total[:, :width] * inv_rms
    up = total[:, width : 2 * width] * inv_rms
    out_ref[...] = (gate / (1.0 + jnp.exp(-gate)) * up).astype(BF16)


def activate(parts):
    rows, wide = parts[0].shape
    return pl.pallas_call(
        activate_kernel,
        out_shape=jax.ShapeDtypeStruct((rows, (wide - 128) // 2), BF16),
        in_specs=[SPEC_VMEM] * len(parts),
        out_specs=SPEC_VMEM,
        compiler_params=pltpu.CompilerParams(vmem_limit_bytes=4 * MIB),
        name="activate",
    )(*parts)


def assemble_kernel(mine_ref, sibling_ref, out_ref):
    half = mine_ref.shape[1]
    left = lax.rem(lax.axis_index("kv"), 2) == 0
    mine, sibling = mine_ref[...].astype(F32), sibling_ref[...].astype(F32)
    out_ref[:, :half] = jnp.where(left, mine, sibling).astype(BF16)
    out_ref[:, half:] = jnp.where(left, sibling, mine).astype(BF16)


def assemble(mine, sibling):
    rows, half = mine.shape
    return pl.pallas_call(
        assemble_kernel,
        out_shape=jax.ShapeDtypeStruct((rows, 2 * half), BF16),
        in_specs=[SPEC_VMEM] * 2,
        out_specs=SPEC_VMEM,
        compiler_params=pltpu.CompilerParams(vmem_limit_bytes=4 * MIB),
        name="assemble",
    )(mine, sibling)


def partner(array, axis, flip):
    pairs = [(i, i ^ flip) for i in range(lax.axis_size(axis))]
    return lax.ppermute(array, axis, pairs)


def swap(parts, axis, unit, flips):
    return [partner(parts[k], axis, k * unit) if k else parts[0] for k in flips]


def line_flips(count):
    return [*range(2, count), 1, 0]


def grid_flips(count):
    return list(range(count - 1, -1, -1))


def sum_over_kv(weight, parts, flips, base, name):
    chips = lax.axis_size("kv") // 2
    mine, theirs = project(weight, parts, flips, name)
    pair = add_pair(mine, partner(theirs, "kv", 1))
    half = add_chips(base, swap([pair] * chips, "kv", 2, range(chips)), name + "_sum")
    return half, partner(half, "kv", 1)


def on_device_tiled(
    queries, drafts, cache, lengths, row_seq, row_pos, w_uv, w_out, hidden, gain, w_gate, w_up, w_down
):
    kv_count = lax.axis_size("kv")
    dp_count = lax.axis_size("dp")
    rows_in, head_count = queries.shape[:2]
    flips = line_flips(dp_count)
    query_t = jnp.swapaxes(queries, 1, 2)
    key_t = jnp.swapaxes(cache, 1, 2)
    mine, theirs, w_uv, w_out, w_gate, w_up = attention(
        kv_count, lengths, row_seq, row_pos, drafts, query_t, key_t, [w_uv, w_out, w_gate, w_up]
    )
    blocks = merge_pair(rows_in, head_count // kv_count, mine, partner(theirs, "kv", 1))
    values = merge_values(rows_in, w_uv, swap(blocks, "kv", 2, grid_flips(len(blocks))))
    resid, resid_sibling = sum_over_kv(w_out, swap([values] * dp_count, "dp", 1, flips), flips, hidden, "project_out")
    sums = expand(dp_count, w_gate, w_up, gain, resid, resid_sibling)
    act = activate(swap(sums, "dp", 1, flips))
    mixed, mixed_sibling = sum_over_kv(w_down, swap([act] * dp_count, "dp", 1, flips), flips, resid, "project_down")
    return assemble(mixed, mixed_sibling)


def tiles_fit(kv_count, dp_count, head_count, rows_in, cols, ctx):
    powers = kv_count & (kv_count - 1) == 0 and dp_count & (dp_count - 1) == 0
    heads = head_count % (16 * kv_count) == 0 and head_count == 128 and kv_count * rows_in <= 128
    return powers and heads and rows_in == 8 and cols % 256 == 0 and ctx % (2 * CHUNK) == 0


def solution(mesh):
    placed = (
        P("dp", None, None),
        P("dp", None),
        P("dp", "kv", None),
        P("dp"),
        P("dp"),
        P("dp"),
        P("kv", None, None),
        P("kv", "dp"),
        P(None, "dp"),
        P("dp"),
        P("dp", "kv"),
        P("dp", "kv"),
        P("kv", "dp"),
    )

    def placed_call(body):
        return jax.shard_map(
            body, mesh=mesh, in_specs=placed, out_specs=P(None, "dp"), check_vma=False
        )

    def run(*args):
        kv_count, dp_count = mesh.shape["kv"], mesh.shape["dp"]
        queries, cache, hidden = args[0], args[2], args[8]
        fits = tiles_fit(
            kv_count,
            dp_count,
            queries.shape[1],
            queries.shape[0] // dp_count,
            hidden.shape[1] // dp_count,
            cache.shape[1] // kv_count,
        )
        return placed_call(on_device_tiled if fits else on_device)(*args)

    return run
```
